512 devices in a mesh: ax: 32 (over y_lo, z), sec: 16 (over x, y_hi, core).
Axes of the slice: x: 4, y: 8 (y_hi: 2, y_lo: 4; y = y_hi * 4 + y_lo), z: 8, core: 2. Of those that a mesh axis runs over, the one named last changes fastest.
Arguments:
- balance_quantities: float32 [5, 128, 512, 128], P(None, 'ax', 'sec'), may hold values from -0.75 to 3.5, as said below
- register: float32 [5, 128, 512, 128], P(None, 'ax', 'sec'), may hold values from -6 to 6
Outputs:
- conserved_new: float32 [5, 128, 512, 128], P(None, 'ax', 'sec')
- register_new: float32 [5, 128, 512, 128], P(None, 'ax', 'sec')
The draws below stay inside these ranges and needn't reach their ends.
Inputs may be any that keep to these rules, and one draw needn't show every extreme that they name: `balance_quantities`: component 0 lies in 0.5 to 1.5 and component 4 in 1.5 to 3.5; components 1 to 3 vanish at the first and last radial nodes.
All inputs are finite; a program needn't handle non-finite values.
Results may differ from the reference program's by a relative error of at most 0.0004.
Values sent between devices are 32-bit elements; how exact they have to be, the bound alone decides.
A program may use at most 64 MiB of HBM per device.

```python
import jax
import jax.numpy as jnp
from jax import lax

R = 128
NTH = 512
NZ = 128


desired_bulk_speed = 0.4


def draw_balance_quantities(key, part):
    noise = jnp.clip(jax.random.normal(key, (5, NZ, NTH, R), jnp.float32), -5.0, 5.0)
    nodes = jnp.cos(jnp.pi * jnp.arange(R).astype(jnp.float32) / (R - 1))
    envelope = 1.0 - nodes * nodes
    plane_noise = jax.random.uniform(jax.random.fold_in(key, 101), (NZ,), jnp.float32, -1.0, 1.0)
    sign_choice = (2 * jax.random.randint(jax.random.fold_in(key, 102), (), 0, 2) - 1).astype(jnp.float32)
    offset = 0.015 + 0.01 * jax.random.uniform(jax.random.fold_in(key, 103), (), jnp.float32)
    bulk_level = desired_bulk_speed * (2.0 * R / (R - 1.0)) * (1.0 + sign_choice * offset)
    profile = 0.5 + (jnp.arange(NZ).astype(jnp.float32) + 0.5) / NZ
    plane_level = bulk_level * profile * (1.0 + 0.15 * plane_noise)
    specific_volume_inverse = 1.0 + 0.1 * noise[0]
    streamwise_momentum = (plane_level[:, None, None] + 0.15 * noise[1]) * envelope
    azim_momentum = 0.15 * noise[2] * envelope
    radial_momentum = 0.15 * noise[3] * envelope
    energy = 2.5 + 0.2 * noise[4]
    return jnp.stack([specific_volume_inverse, streamwise_momentum, azim_momentum, radial_momentum, energy]).astype(jnp.float32)


def level_of(stream_key, dims, shards, smallest, high):
    factor_of, own = 1.0, jax.random.fold_in(stream_key, 6)
    for axis_at, shards_of in shards:
        steps = jnp.exp(jax.random.uniform(jax.random.fold_in(own, axis_at), (shards_of,), jnp.float32, smallest / len(shards), high / len(shards)))
        factor_of = factor_of * jnp.repeat(steps, dims[axis_at] // shards_of).reshape([-1 if axis == axis_at else 1 for axis in range(len(dims))])
    return factor_of


def centred(rng, shape, scale, limit, shards=(), dtype=jnp.bfloat16):
    drawn = jax.random.normal(rng, shape, jnp.float32) * scale
    if len(shards) > 0:
        drawn = level_of(rng, shape, shards, -0.22, 0.18) * drawn
    return jnp.clip(drawn, min=-limit, max=limit).astype(dtype)


def setup_inputs(seed: int = 0) -> dict:
    key_list = jax.random.split(jax.random.key(seed), 3)
    return {
        "balance_quantities": draw_balance_quantities(jax.random.fold_in(key_list[2], 71), 0),
        "register": centred(key_list[1], (5, NZ, NTH, R), 1.0, 6.0, ((1, 32), (2, 16)), jnp.float32),
    }


HEAT_RATIO = 1.4
AXIAL_STEP = 0.003
INNER_RADIUS = 0.25
TIME_STEP = 1e-3
SECTION_DECAY = -5.0 / 9.0
SEGMENT_WEIGHT = 15.0 / 16.0
VISCOSITY = 2.5e-5
CONDUCTION = VISCOSITY / ((HEAT_RATIO - 1.0) * 0.7)
TARGET_BULK = 0.4
FORCE_RATE = 8000.0
FIRST_COEFFS = (4.0 / 5.0, -1.0 / 5.0, 4.0 / 105.0, -1.0 / 280.0)
SECOND_CENTER = -205.0 / 72.0
SECOND_COEFFS = (8.0 / 5.0, -1.0 / 5.0, 8.0 / 315.0, -1.0 / 560.0)
HIGHEST = lax.Precision.HIGHEST


def radial_matrix(number_of_shells):
    positions = jnp.arange(number_of_shells)
    nodes = jnp.cos(jnp.pi * positions.astype(jnp.float32) / (number_of_shells - 1))
    radius = 0.5 * (1.0 + INNER_RADIUS) + 0.5 * (1.0 - INNER_RADIUS) * nodes
    row_index = positions[:, None]
    col_index = positions[None, :]
    endpoint = jnp.where((positions == 0) | (positions == number_of_shells - 1), 2.0, 1.0).astype(jnp.float32)
    parity = jnp.where((row_index + col_index) % 2 == 0, 1.0, -1.0).astype(jnp.float32)
    diagonal = row_index == col_index
    spread = jnp.where(diagonal, 1.0, nodes[:, None] - nodes[None, :])
    offdiag = jnp.where(diagonal, 0.0, endpoint[:, None] / endpoint[None, :] * parity / spread)
    radial_first = (offdiag - jnp.diag(jnp.sum(offdiag, axis=1))) * (2.0 / (1.0 - INNER_RADIUS))
    radial_second = jnp.dot(radial_first, radial_first, precision=HIGHEST)
    return radius, radial_first, radial_second


def azimuth_matrices(azim_count):
    positions = jnp.arange(azim_count)
    offset = (positions[:, None] - positions[None, :]) % azim_count
    angle_step = 2.0 * jnp.pi / azim_count
    half_angle = offset.astype(jnp.float32) * angle_step * 0.5
    parity = jnp.where(offset % 2 == 0, 1.0, -1.0).astype(jnp.float32)
    at_zero = offset == 0
    tangent = jnp.tan(jnp.where(at_zero, 1.0, half_angle))
    azim_first = jnp.where(at_zero, 0.0, 0.5 * parity / tangent)
    sine_value = jnp.sin(jnp.where(at_zero, 1.0, half_angle))
    azim_second = jnp.where(at_zero, -jnp.pi * jnp.pi / (3.0 * angle_step * angle_step) - 1.0 / 6.0,
                            -0.5 * parity / (sine_value * sine_value))
    return azim_first, azim_second


def physical_variables(balance_quantities):
    specific_volume_inverse = balance_quantities[0]
    motion_vector = balance_quantities[1:4] / specific_volume_inverse
    thermodynamic_stress = (HEAT_RATIO - 1.0) * (balance_quantities[4] - 0.5 * jnp.sum(balance_quantities[1:4] * motion_vector, axis=0))
    thermal_state_value = thermodynamic_stress / specific_volume_inverse
    return specific_volume_inverse, motion_vector, thermodynamic_stress, thermal_state_value


def transport_rates(balance_quantities, direction):
    specific_volume_inverse, motion_vector, thermodynamic_stress, thermal_state_value = physical_variables(balance_quantities)
    along_speed = motion_vector[direction]
    pieces = [balance_quantities[component] * along_speed for component in range(5)]
    pieces[1 + direction] = pieces[1 + direction] + thermodynamic_stress
    pieces[4] = pieces[4] + thermodynamic_stress * along_speed
    return jnp.stack(pieces)


def transported(balance_quantities):
    specific_volume_inverse, motion_vector, thermodynamic_stress, thermal_state_value = physical_variables(balance_quantities)
    return jnp.concatenate([motion_vector, thermal_state_value[None]], axis=0)


def axial_parts(balance_quantities):
    return jnp.concatenate([transport_rates(balance_quantities, 0), transported(balance_quantities)], axis=0)


def azim_parts(balance_quantities):
    return jnp.concatenate([transport_rates(balance_quantities, 1), transported(balance_quantities)], axis=0)


def assemble(balance_quantities, motion_vector, thermodynamic_stress, convect, lap, forcing, radius):
    terms = [-convect[0],
             -convect[1] + VISCOSITY * lap[0] + forcing,
             -convect[2] - balance_quantities[2] * motion_vector[2] / radius + VISCOSITY * lap[1],
             -convect[3] + (balance_quantities[2] * motion_vector[1] + thermodynamic_stress) / radius + VISCOSITY * lap[2],
             -convect[4] + CONDUCTION * lap[3] + forcing * motion_vector[0]]
    return jnp.stack(terms)


def reference(balance_quantities, register):
    radius, radial_first, radial_second = radial_matrix(R)
    azim_first, azim_second = azimuth_matrices(NTH)

    def plane_terms(plane):
        stacked = jnp.concatenate([transport_rates(plane, 2) * radius, transported(plane)], axis=0)
        radial_one = jnp.dot(stacked, radial_first.T, precision=HIGHEST)
        radial_two = jnp.dot(stacked[5:], radial_second.T, precision=HIGHEST)
        pieces = azim_parts(plane)
        turn_first = jnp.einsum("ab,cbi->cai", azim_first, pieces[:5], precision=HIGHEST)
        turn_second = jnp.einsum("ab,cbi->cai", azim_second, pieces[5:], precision=HIGHEST)
        convect_part = radial_one[:5] / radius + turn_first / radius
        lap_part = radial_two + radial_one[5:] / radius + turn_second / (radius * radius)
        return jnp.concatenate([convect_part, lap_part], axis=0)

    planar = lax.map(plane_terms, jnp.moveaxis(balance_quantities, 1, 0))
    planar = jnp.moveaxis(planar, 0, 1)
    pieces = axial_parts(balance_quantities)
    axial_one = jnp.zeros_like(pieces[:5])
    for offset, weight in enumerate(FIRST_COEFFS, 1):
        axial_one = axial_one + weight * (jnp.roll(pieces[:5], -offset, axis=1) - jnp.roll(pieces[:5], offset, axis=1))
    axial_one = axial_one / AXIAL_STEP
    axial_two = SECOND_CENTER * pieces[5:]
    for offset, weight in enumerate(SECOND_COEFFS, 1):
        axial_two = axial_two + weight * (jnp.roll(pieces[5:], -offset, axis=1) + jnp.roll(pieces[5:], offset, axis=1))
    axial_two = axial_two / (AXIAL_STEP * AXIAL_STEP)
    convect = axial_one + planar[:5]
    lap = planar[5:] + axial_two
    specific_volume_inverse, motion_vector, thermodynamic_stress, thermal_state_value = physical_variables(balance_quantities)
    bulk_mean = jnp.sum(balance_quantities[1] * radius) / (NZ * NTH * jnp.sum(radius))
    forcing = FORCE_RATE * (TARGET_BULK - bulk_mean)
    tendency = assemble(balance_quantities, motion_vector, thermodynamic_stress, convect, lap, forcing, radius)
    register_new = SECTION_DECAY * register + TIME_STEP * tendency
    conserved_new = balance_quantities + SEGMENT_WEIGHT * register_new
    return (conserved_new, register_new)
```

```python
import functools

import jax
import jax.numpy as jnp
import ml_dtypes
import numpy as np
from jax import lax
from jax.experimental import pallas as pl
from jax.experimental.pallas import tpu as pltpu
from jax.sharding import PartitionSpec as P

AXIAL_STEP = 0.003
TIME_STEP = 0.001
SECTION_DECAY = -5.0 / 9.0
SEGMENT_WEIGHT = 15.0 / 16.0
VISCOSITY = 2.5e-05
CONDUCTION = VISCOSITY / (0.4 * 0.7)
TARGET_BULK = 0.4
FORCE_RATE = 8000.0
FIRST_COEFFS = (4.0 / 5.0, -1.0 / 5.0, 4.0 / 105.0, -1.0 / 280.0)
SECOND_CENTER = -205.0 / 72.0
SECOND_COEFFS = (8.0 / 5.0, -1.0 / 5.0, 8.0 / 315.0, -1.0 / 560.0)
HIGHEST = lax.Precision.HIGHEST
MESH = pl.DeviceIdType.MESH

R = 128
NTH = 512
NZ = 128
NSEC = 16
NAX = 32
F32 = jnp.float32
BF16 = jnp.bfloat16


def constants():
    index = np.arange(R)
    nodes = np.cos(np.pi * index / (R - 1))
    radius = 0.625 + 0.375 * nodes
    ends = np.where((index == 0) | (index == R - 1), 2.0, 1.0)
    spread = nodes[:, None] - nodes[None, :]
    np.fill_diagonal(spread, 1.0)
    parity = np.where((index[:, None] + index[None, :]) % 2 == 0, 1.0, -1.0)
    off = ends[:, None] / ends[None, :] * parity / spread
    np.fill_diagonal(off, 0.0)
    first = (off - np.diag(off.sum(axis=1))) * (2.0 / 0.75)
    second = first @ first

    lag = (np.arange(NTH)[:, None] - np.arange(NTH)[None, :]) % NTH
    step = 2.0 * np.pi / NTH
    sign = np.where(lag % 2 == 0, 1.0, -1.0)
    safe = np.where(lag == 0, 1, lag)
    azim_first = np.where(lag == 0, 0.0, 0.5 * sign / np.tan(safe * step / 2))
    azim_second = np.where(
        lag == 0,
        -np.pi * np.pi / (3.0 * step * step) - 1.0 / 6.0,
        -0.5 * sign / np.sin(safe * step / 2) ** 2,
    )
    order = (
        np.arange(NTH).reshape(NSEC, 4, 8).transpose(1, 0, 2).reshape(NTH)
    )
    both = np.concatenate(
        [azim_first[order][:, order], azim_second[order][:, order]], axis=1
    )
    both = both.astype(np.float32)
    high = both.astype(ml_dtypes.bfloat16)
    low = (both - high.astype(np.float32)).astype(ml_dtypes.bfloat16)

    flux_op = -TIME_STEP * (first * radius[None, :]) / radius[:, None]
    diff_op = TIME_STEP * (second + first / radius[:, None])
    radial = np.stack(
        [flux_op.T, VISCOSITY * diff_op.T, CONDUCTION * diff_op.T]
    ).astype(np.float32)

    rows = np.zeros((8, R), np.float32)
    rows[0] = radius
    rows[1] = 1.0 / radius
    quarter = np.zeros((4, 8, R), np.float32)
    for q in range(4):
        own = np.tile(radius[32 * q : 32 * q + 32], 4)
        quarter[q, 0] = -TIME_STEP / own
        quarter[q, 1] = TIME_STEP * VISCOSITY / own**2
        quarter[q, 2] = TIME_STEP * CONDUCTION / own**2
    scale = 1.0 / (NZ * NTH * radius.sum())
    return high, low, radial, rows, quarter, float(scale)


def block_transpose(v, lane):
    v0, v1, v2, v3 = v
    low = lane < 64
    even = (lane // 32) % 2 == 0

    def swap(a, b, mask, shift):
        return (
            jnp.where(mask, a, pltpu.roll(b, shift, 1)),
            jnp.where(mask, pltpu.roll(a, 128 - shift, 1), b),
        )

    a0, a2 = swap(v0, v2, low, 64)
    a1, a3 = swap(v1, v3, low, 64)
    b0, b1 = swap(a0, a1, even, 32)
    b2, b3 = swap(a2, a3, even, 32)
    return b0, b1, b2, b3


def physical(q):
    inverse = 1.0 / q[0]
    v = [q[1] * inverse, q[2] * inverse, q[3] * inverse]
    pressure = 0.4 * (q[4] - 0.5 * (q[1] * v[0] + q[2] * v[1] + q[3] * v[2]))
    return v, pressure, pressure * inverse


def flux(q, v, pressure, direction):
    w = v[direction]
    out = [q[1 + direction], q[1] * w, q[2] * w, q[3] * w, (q[4] + pressure) * w]
    out[1 + direction] = out[1 + direction] + pressure
    return out


def split(x):
    high = x.astype(BF16)
    return high, (x - high.astype(F32)).astype(BF16)


def body(
    scale,
    q_ref,
    high_hbm,
    low_hbm,
    radial_ref,
    rows_ref,
    quarter_ref,
    out_ref,
    high,
    low,
    pack,
    recv,
    send,
    back,
    halo,
    sums,
    pairs,
    totals,
    load_sem,
    a_send,
    a_recv,
    s_send,
    s_recv,
    p_send,
    p_recv,
    b_send,
    b_recv,
    t_send,
    t_recv,
    h_send,
    h_recv,
):
    ax = lax.axis_index("ax")
    sec = lax.axis_index("sec")
    loads = [
        pltpu.make_async_copy(high_hbm, high, load_sem.at[0]),
        pltpu.make_async_copy(low_hbm, low, load_sem.at[1]),
    ]
    for copy in loads:
        copy.start()

    def remote(src, dst, send_sem, recv_sem, to_ax, to_sec):
        return pltpu.make_async_remote_copy(
            src_ref=src,
            dst_ref=dst,
            send_sem=send_sem,
            recv_sem=recv_sem,
            device_id=(to_ax, to_sec),
            device_id_type=MESH,
        )

    right = lax.rem(ax + 1, NAX)
    left = lax.rem(ax + NAX - 1, NAX)
    near, far = 2 * sec + 1, 2 * sec + 2
    last = sec == NSEC - 1

    barrier = pltpu.get_barrier_semaphore()

    def greet(to_ax, to_sec):
        pl.semaphore_signal(
            barrier, inc=1, device_id=(to_ax, to_sec), device_id_type=MESH
        )

    peers = [lax.rem(sec + d, NSEC) for d in range(1, NSEC)]
    for peer in peers:
        greet(ax, peer)
    greet(left, sec)
    greet(right, sec)
    greet(lax.rem(ax + near, NAX), sec)

    @pl.when(jnp.logical_not(last))
    def _():
        greet(lax.rem(ax + far, NAX), sec)

    lane = lax.broadcasted_iota(jnp.int32, (1, 128), 1)
    groups = [
        q_ref[:, :, 8 * g : 8 * g + 8, :].reshape(160, 128) for g in range(4)
    ]
    for quarter, packed in enumerate(block_transpose(groups, lane)):
        packed = packed.reshape(5, 4, 8, 128)
        for plane in range(4):
            pack[4 * plane + quarter] = packed[:, plane]

    radius = rows_ref[0:1, :]
    flow = jnp.sum(q_ref[1].reshape(128, 128) * radius, axis=0, keepdims=True)
    sums[sec] = flow

    pl.semaphore_wait(barrier, jnp.where(last, 18, 19))

    first = []
    for d, peer in enumerate(peers):
        first.append(
            remote(sums.at[sec], sums.at[sec], s_send.at[d], s_recv.at[d], ax, peer)
        )
        first.append(
            remote(pack.at[peer], recv.at[sec], a_send.at[d], a_recv.at[d], ax, peer)
        )
    for copy in first:
        copy.start()
    recv[sec] = pack[sec]
    halos = [
        remote(q_ref, halo.at[0], h_send.at[0], h_recv.at[0], right, sec),
        remote(q_ref, halo.at[1], h_send.at[1], h_recv.at[1], left, sec),
    ]
    for copy in halos:
        copy.start()

    whole = [q_ref[c].reshape(128, 128) for c in range(5)]
    v, pressure, heat = physical(whole)
    inverse_radius = rows_ref[1:2, :]
    diffused = v + [heat]
    tend = []
    for c, field in enumerate(flux(whole, v, pressure, 2)):
        value = jnp.dot(
            field, radial_ref[0], precision=HIGHEST, preferred_element_type=F32
        )
        if c:
            value = value + jnp.dot(
                diffused[c - 1],
                radial_ref[2 if c == 4 else 1],
                precision=HIGHEST,
                preferred_element_type=F32,
            )
        tend.append(value)
    turn = TIME_STEP * inverse_radius
    tend[2] = tend[2] - whole[2] * v[2] * turn
    tend[3] = tend[3] + (whole[2] * v[1] + pressure) * turn
    for c in range(5):
        out_ref[c] = tend[c].reshape(4, 32, 128)

    for copy in first[0::2]:
        copy.wait_recv()
    slab = sums[0]
    for s in range(1, NSEC):
        slab = slab + sums[s]
    pairs[0] = slab
    ring_near = remote(
        pairs.at[0],
        pairs.at[1],
        p_send.at[0],
        p_recv.at[0],
        lax.rem(ax + NAX - near, NAX),
        sec,
    )
    ring_far = remote(
        pairs.at[0],
        pairs.at[2],
        p_send.at[1],
        p_recv.at[1],
        lax.rem(ax + 2 * NAX - far, NAX),
        sec,
    )
    ring_near.start()

    @pl.when(jnp.logical_not(last))
    def _():
        ring_far.start()

    for copy in loads:
        copy.wait()
    for copy in first[1::2]:
        copy.wait_recv()
    lines = [recv[:, c].reshape(128, 128) for c in range(5)]
    v, pressure, heat = physical(lines)
    mine = quarter_ref[lax.rem(sec, 4)]
    fields = [f * mine[0:1] for f in flux(lines, v, pressure, 1)]
    viscous = [u * mine[1:2] for u in v] + [heat * mine[2:3]]
    flux_rows = block_transpose(fields[1:], lane)
    viscous_rows = block_transpose(viscous, lane)
    flux_high, flux_low = split(
        jnp.concatenate(
            [
                jnp.concatenate(flux_rows, axis=0),
                jnp.concatenate(
                    [fields[0]]
                    + [pltpu.roll(fields[0], 128 - 32 * g, 1) for g in range(1, 4)],
                    axis=0,
                ),
            ],
            axis=1,
        )
    )
    visc_high, visc_low = split(jnp.concatenate(viscous_rows, axis=0))

    def product(rows, columns, x_high, x_low):
        def dot(a, b):
            return jnp.dot(a[rows, columns], b, preferred_element_type=F32)

        return dot(high, x_high) + (dot(high, x_low) + dot(low, x_high))

    turned = []
    edge = []
    for g in range(4):
        rows = slice(128 * g, 128 * g + 128)
        wide = product(rows, slice(0, 512), flux_high, flux_low)
        thin = product(rows, slice(512, 1024), visc_high, visc_low)
        turned.append(wide[:, :128] + thin)
        edge.append(wide[:, 128:])
    plain = edge[0]
    for g in range(1, 4):
        plain = jnp.where(lane // 32 == g, pltpu.roll(edge[g], 32 * g, 1), plain)
    for c, value in enumerate((plain,) + tuple(block_transpose(turned, lane))):
        send[:, c] = value.reshape(NSEC, 8, 128)

    ring_near.wait_recv()

    @pl.when(jnp.logical_not(last))
    def _():
        ring_far.wait_recv()

    @pl.when(last)
    def _():
        pairs[2] = pairs[0]

    totals[sec] = pairs[1] + pairs[2]
    second = []
    for d, peer in enumerate(peers):
        second.append(
            remote(send.at[peer], back.at[sec], b_send.at[d], b_recv.at[d], ax, peer)
        )
        second.append(
            remote(
                totals.at[sec], totals.at[sec], t_send.at[d], t_recv.at[d], ax, peer
            )
        )
    for copy in second:
        copy.start()
    back[sec] = send[sec]

    for copy in halos:
        copy.wait_recv()
    planes_flux, planes_visc = [], []
    for block in (halo.at[0], q_ref, halo.at[1]):
        cells = [block[c].reshape(128, 128) for c in range(5)]
        v, pressure, heat = physical(cells)
        fields = [f.reshape(4, 32, 128) for f in flux(cells, v, pressure, 0)]
        others = [f.reshape(4, 32, 128) for f in v + [heat]]
        for plane in range(4):
            planes_flux.append([f[plane] for f in fields])
            planes_visc.append([f[plane] for f in others])
    for plane in range(4):
        at = plane + 4
        for c in range(5):
            value = out_ref[c, plane]
            for k in range(1, 5):
                weight = -TIME_STEP * FIRST_COEFFS[k - 1] / AXIAL_STEP
                value = value + weight * (
                    planes_flux[at + k][c] - planes_flux[at - k][c]
                )
            if c:
                factor = (CONDUCTION if c == 4 else VISCOSITY) * TIME_STEP
                factor = factor / (AXIAL_STEP * AXIAL_STEP)
                value = value + factor * SECOND_CENTER * planes_visc[at][c - 1]
                for k in range(1, 5):
                    value = value + factor * SECOND_COEFFS[k - 1] * (
                        planes_visc[at + k][c - 1] + planes_visc[at - k][c - 1]
                    )
            out_ref[c, plane] = value

    for copy in second:
        copy.wait_recv()
    total = totals[0]
    for s in range(1, NSEC):
        total = total + totals[s]
    bulk = jnp.sum(total, axis=1, keepdims=True) * scale
    forcing = (TIME_STEP * FORCE_RATE) * (TARGET_BULK - bulk)
    ret = [
        jnp.stack([back[4 * p + quarter] for p in range(4)]).reshape(160, 128)
        for quarter in range(4)
    ]
    for g, value in enumerate(block_transpose(ret, lane)):
        value = value.reshape(4, 5, 8, 128)
        rows = slice(8 * g, 8 * g + 8)
        for c in range(5):
            more = value[:, c]
            if c == 1:
                more = more + forcing.reshape(1, 1, 1)
            if c == 4:
                more = more + forcing.reshape(1, 1, 1) * (
                    q_ref[1, :, rows, :] / q_ref[0, :, rows, :]
                )
            out_ref[c, :, rows, :] = out_ref[c, :, rows, :] + more

    for copy in first + second + halos + [ring_near]:
        copy.wait_send()

    @pl.when(jnp.logical_not(last))
    def _():
        ring_far.wait_send()


def solution(mesh):
    high, low, radial, rows, quarter, scale = constants()

    def shards(balance_quantities, register):
        vmem = pl.BlockSpec(memory_space=pltpu.VMEM)
        hbm = pl.BlockSpec(memory_space=pl.ANY)
        dma = pltpu.SemaphoreType.DMA
        tendency = pl.pallas_call(
            functools.partial(body, scale),
            out_shape=jax.ShapeDtypeStruct((5, 4, 32, R), F32),
            in_specs=[vmem, hbm, hbm, vmem, vmem, vmem],
            out_specs=vmem,
            scratch_shapes=[
                pltpu.VMEM((NTH, 2 * NTH), BF16),
                pltpu.VMEM((NTH, 2 * NTH), BF16),
                pltpu.VMEM((NSEC, 5, 8, 128), F32),
                pltpu.VMEM((NSEC, 5, 8, 128), F32),
                pltpu.VMEM((NSEC, 5, 8, 128), F32),
                pltpu.VMEM((NSEC, 5, 8, 128), F32),
                pltpu.VMEM((2, 5, 4, 32, R), F32),
                pltpu.VMEM((NSEC, 1, 128), F32),
                pltpu.VMEM((3, 1, 128), F32),
                pltpu.VMEM((NSEC, 1, 128), F32),
                dma((2,)),
                dma((15,)),
                dma((15,)),
                dma((15,)),
                dma((15,)),
                dma((2,)),
                dma((2,)),
                dma((15,)),
                dma((15,)),
                dma((15,)),
                dma((15,)),
                dma((2,)),
                dma((2,)),
            ],
            compiler_params=pltpu.CompilerParams(
                collective_id=0,
                has_side_effects=True,
                vmem_limit_bytes=40 * 1024 * 1024,
            ),
        )(balance_quantities, high, low, radial, rows, quarter)
        register_new = SECTION_DECAY * register + tendency
        conserved_new = balance_quantities + SEGMENT_WEIGHT * register_new
        return conserved_new, register_new

    spec = P(None, "ax", "sec", None)
    return jax.shard_map(
        shards,
        mesh=mesh,
        in_specs=(spec, spec),
        out_specs=(spec, spec),
        check_vma=False,
    )
```

```python
import functools

import jax
import jax.numpy as jnp
import ml_dtypes
import numpy as np
from jax import lax
from jax.experimental import pallas as pl
from jax.experimental.pallas import tpu as pltpu
from jax.sharding import PartitionSpec as P

AXIAL_STEP = 0.003
TIME_STEP = 0.001
SECTION_DECAY = -5.0 / 9.0
SEGMENT_WEIGHT = 15.0 / 16.0
VISCOSITY = 2.5e-05
CONDUCTION = VISCOSITY / (0.4 * 0.7)
TARGET_BULK = 0.4
FORCE_RATE = 8000.0
FIRST_COEFFS = (4.0 / 5.0, -1.0 / 5.0, 4.0 / 105.0, -1.0 / 280.0)
SECOND_CENTER = -205.0 / 72.0
SECOND_COEFFS = (8.0 / 5.0, -1.0 / 5.0, 8.0 / 315.0, -1.0 / 560.0)
HIGHEST = lax.Precision.HIGHEST
MESH = pl.DeviceIdType.MESH

R = 128
NTH = 512
NZ = 128
NSEC = 16
NAX = 32
F32 = jnp.float32
BF16 = jnp.bfloat16


def constants():
    index = np.arange(R)
    nodes = np.cos(np.pi * index / (R - 1))
    radius = 0.625 + 0.375 * nodes
    ends = np.where((index == 0) | (index == R - 1), 2.0, 1.0)
    spread = nodes[:, None] - nodes[None, :]
    np.fill_diagonal(spread, 1.0)
    parity = np.where((index[:, None] + index[None, :]) % 2 == 0, 1.0, -1.0)
    off = ends[:, None] / ends[None, :] * parity / spread
    np.fill_diagonal(off, 0.0)
    first = (off - np.diag(off.sum(axis=1))) * (2.0 / 0.75)
    second = first @ first

    lag = (np.arange(NTH)[:, None] - np.arange(NTH)[None, :]) % NTH
    step = 2.0 * np.pi / NTH
    sign = np.where(lag % 2 == 0, 1.0, -1.0)
    safe = np.where(lag == 0, 1, lag)
    azim_first = np.where(lag == 0, 0.0, 0.5 * sign / np.tan(safe * step / 2))
    azim_second = np.where(
        lag == 0,
        -np.pi * np.pi / (3.0 * step * step) - 1.0 / 6.0,
        -0.5 * sign / np.sin(safe * step / 2) ** 2,
    )
    order = np.arange(NTH).reshape(4, 2, 2, 4, 8).transpose(1, 3, 0, 2, 4).reshape(NTH)
    both = np.stack([azim_first[order][:, order], azim_second[order][:, order]])
    both = both.reshape(2, 2, 256, 2, 256).transpose(1, 3, 0, 2, 4)
    both = both.astype(np.float32)
    high = both.astype(ml_dtypes.bfloat16)
    low = (both - high.astype(np.float32)).astype(ml_dtypes.bfloat16)

    flux_op = -TIME_STEP * (first * radius[None, :]) / radius[:, None]
    diff_op = TIME_STEP * (second + first / radius[:, None])
    radial = np.stack(
        [flux_op.T, VISCOSITY * diff_op.T, CONDUCTION * diff_op.T]
    ).astype(np.float32)

    rows = np.zeros((8, R), np.float32)
    rows[0] = radius
    rows[1] = 1.0 / radius
    quarter = np.zeros((4, 8, R), np.float32)
    for q in range(4):
        own = np.tile(radius[32 * q : 32 * q + 32], 4)
        quarter[q, 0] = -TIME_STEP / own
        quarter[q, 1] = TIME_STEP * VISCOSITY / own**2
        quarter[q, 2] = TIME_STEP * CONDUCTION / own**2
    scale = 1.0 / (NZ * NTH * radius.sum())
    return high, low, radial, rows, quarter, float(scale)


def block_transpose(v, lane):
    v0, v1, v2, v3 = v
    low = lane < 64
    even = (lane // 32) % 2 == 0

    def swap(a, b, mask, shift):
        return (
            jnp.where(mask, a, pltpu.roll(b, shift, 1)),
            jnp.where(mask, pltpu.roll(a, 128 - shift, 1), b),
        )

    a0, a2 = swap(v0, v2, low, 64)
    a1, a3 = swap(v1, v3, low, 64)
    b0, b1 = swap(a0, a1, even, 32)
    b2, b3 = swap(a2, a3, even, 32)
    return b0, b1, b2, b3


def physical(q):
    inverse = 1.0 / q[0]
    v = [q[1] * inverse, q[2] * inverse, q[3] * inverse]
    pressure = 0.4 * (q[4] - 0.5 * (q[1] * v[0] + q[2] * v[1] + q[3] * v[2]))
    return v, pressure, pressure * inverse


def flux(q, v, pressure, direction):
    w = v[direction]
    out = [q[1 + direction], q[1] * w, q[2] * w, q[3] * w, (q[4] + pressure) * w]
    out[1 + direction] = out[1 + direction] + pressure
    return out


def split(x):
    high = x.astype(BF16)
    return high, (x - high.astype(F32)).astype(BF16)


def body(
    scale,
    q_hbm,
    high_hbm,
    low_hbm,
    radial_hbm,
    rows_hbm,
    quarter_hbm,
    out_ref,
    q_ref,
    high,
    low,
    radial_ref,
    rows_ref,
    quarter_ref,
    pack,
    recv,
    send,
    back,
    halo,
    sums,
    pairs,
    totals,
    load_sem,
    a_send,
    a_recv,
    s_send,
    s_recv,
    p_send,
    p_recv,
    b_send,
    b_recv,
    t_send,
    t_recv,
    h_send,
    h_recv,
    halo_ready,
    ring_ready,
):
    ax = lax.axis_index("ax")
    sec = lax.axis_index("sec")
    x, half, core = sec // 4, lax.rem(sec // 2, 2), lax.rem(sec, 2)
    me = 8 * half + 2 * x + core

    def remote(src, dst, send_sem, recv_sem, to_ax, to_sec):
        return pltpu.make_async_remote_copy(
            src_ref=src,
            dst_ref=dst,
            send_sem=send_sem,
            recv_sem=recv_sem,
            device_id=(to_ax, to_sec),
            device_id_type=MESH,
        )

    def at_sector(to_x, to_half, to_core):
        return 4 * to_x + 2 * to_half + to_core, 8 * to_half + 2 * to_x + to_core

    def shifted(dx):
        return lax.rem(x + dx, 4)

    far_peers = [
        at_sector(shifted(dx), 1 - half, c) for c in range(2) for dx in (2, 1, 3, 0)
    ]
    near_peers = [
        at_sector(shifted(dx), half, c) for c in range(2) for dx in (2, 1, 3)
    ] + [at_sector(x, half, 1 - core)]
    ordered = far_peers[:4] + near_peers[:3] + far_peers[4:] + near_peers[3:]

    plane_at = lax.rem(ax, 8)
    right = lax.rem(ax + 1, NAX)
    left = lax.rem(ax + NAX - 1, NAX)

    def rank(at):
        return 4 * lax.rem(at, 8) + at // 8

    mine_rank = rank(ax)
    offsets = [2 * sec + 1, 2 * sec + 2]
    valid = [sec >= 0, sec < NSEC - 1]
    targets = [lax.rem(ax + 2 * NAX - o, NAX) for o in offsets]
    sources = [lax.rem(ax + o, NAX) for o in offsets]
    target_lower = [rank(t) < mine_rank for t in targets]
    source_lower = [rank(t) < mine_rank for t in sources]

    def both(a, b):
        return jnp.logical_and(a, b)

    def signal(sem, to_ax, to_sec):
        pl.semaphore_signal(
            sem, inc=1, device_id=(to_ax, to_sec), device_id_type=MESH
        )

    barrier = pltpu.get_barrier_semaphore()
    loads = [
        pltpu.make_async_copy(src, dst, load_sem.at[i])
        for i, (src, dst) in enumerate(
            (
                (q_hbm, q_ref),
                (rows_hbm, rows_ref),
                (quarter_hbm, quarter_ref),
                (radial_hbm, radial_ref),
                (high_hbm, high),
                (low_hbm, low),
            )
        )
    ]
    loads[0].start()
    loads[1].start()
    for peer, _ in ordered:
        signal(barrier, ax, peer)

    @pl.when(plane_at != 7)
    def _():
        signal(barrier, right, sec)

    @pl.when(plane_at == 0)
    def _():
        signal(barrier, left, sec)

    count = 15 + jnp.where(plane_at != 0, 1, 0) + jnp.where(plane_at == 7, 1, 0)
    for k in range(2):

        @pl.when(both(valid[k], jnp.logical_not(target_lower[k])))
        def _():
            signal(barrier, targets[k], sec)

        @pl.when(both(valid[k], jnp.logical_not(source_lower[k])))
        def _():
            signal(barrier, sources[k], sec)

        count = count + jnp.where(both(valid[k], target_lower[k]), 1, 0)
        count = count + jnp.where(both(valid[k], source_lower[k]), 1, 0)
    for copy in loads[2:]:
        copy.start()

    loads[0].wait()
    loads[1].wait()
    radius = rows_ref[0:1, :]
    flow = jnp.sum(q_ref[1].reshape(128, 128) * radius, axis=0, keepdims=True)
    sums[me] = flow

    lane = lax.broadcasted_iota(jnp.int32, (1, 128), 1)
    groups = [
        q_ref[:, :, 8 * g : 8 * g + 8, :].reshape(160, 128) for g in range(4)
    ]
    for quarter, packed in enumerate(block_transpose(groups, lane)):
        packed = packed.reshape(5, 4, 8, 128)
        for plane in range(4):
            pack[4 * plane + quarter] = packed[:, plane]

    pl.semaphore_wait(barrier, count)

    def sums_copy(peer, at):
        return remote(sums.at[me], sums.at[me], s_send.at[at], s_recv.at[me], ax, peer)

    def sums_from(at):
        return remote(sums.at[at], sums.at[at], s_send.at[at], s_recv.at[at], ax, sec)

    def pack_copy(peer, at):
        return remote(pack.at[at], recv.at[me], a_send.at[at], a_recv.at[me], ax, peer)

    def pack_from(at):
        return remote(pack.at[at], recv.at[at], a_send.at[at], a_recv.at[at], ax, sec)

    def back_copy(peer, at):
        return remote(send.at[at], back.at[me], b_send.at[at], b_recv.at[me], ax, peer)

    def back_from(at):
        return remote(send.at[at], back.at[at], b_send.at[at], b_recv.at[at], ax, sec)

    def total_copy(peer, at):
        return remote(
            totals.at[me], totals.at[me], t_send.at[at], t_recv.at[me], ax, peer
        )

    def total_from(at):
        return remote(
            totals.at[at], totals.at[at], t_send.at[at], t_recv.at[at], ax, sec
        )

    for peer, at in ordered:
        sums_copy(peer, at).start()
    for peer, at in ordered:
        pack_copy(peer, at).start()

    @pl.when(plane_at != 0)
    def _():
        signal(halo_ready.at[0], left, sec)

    @pl.when(plane_at == 7)
    def _():
        signal(halo_ready.at[1], right, sec)

    for k in range(2):

        @pl.when(both(valid[k], source_lower[k]))
        def _():
            signal(ring_ready.at[k], sources[k], sec)

    to_right = remote(q_ref, halo.at[0], h_send.at[0], h_recv.at[0], right, sec)
    to_left = remote(q_ref, halo.at[1], h_send.at[1], h_recv.at[1], left, sec)

    @pl.when(plane_at != 0)
    def _():
        to_left.start()

    recv[me] = pack[me]

    loads[3].wait()
    whole = [q_ref[c].reshape(128, 128) for c in range(5)]
    v, pressure, heat = physical(whole)
    inverse_radius = rows_ref[1:2, :]
    diffused = v + [heat]
    tend = []
    for c, field in enumerate(flux(whole, v, pressure, 2)):
        value = jnp.dot(
            field, radial_ref[0], precision=HIGHEST, preferred_element_type=F32
        )
        if c:
            value = value + jnp.dot(
                diffused[c - 1],
                radial_ref[2 if c == 4 else 1],
                precision=HIGHEST,
                preferred_element_type=F32,
            )
        tend.append(value)
    turn = TIME_STEP * inverse_radius
    tend[2] = tend[2] - whole[2] * v[2] * turn
    tend[3] = tend[3] + (whole[2] * v[1] + pressure) * turn
    for c in range(5):
        out_ref[c] = tend[c].reshape(4, 32, 128)

    @pl.when(plane_at != 7)
    def _():
        pl.semaphore_wait(halo_ready.at[0], 1)

    to_right.start()

    for _, at in ordered:
        sums_from(at).wait_recv()
    slab = sums[0]
    for s in range(1, NSEC):
        slab = slab + sums[s]
    pairs[0] = slab
    ring = [
        remote(
            pairs.at[0],
            pairs.at[1 + k],
            p_send.at[k],
            p_recv.at[k],
            targets[k],
            sec,
        )
        for k in range(2)
    ]
    for k in range(2):

        @pl.when(both(valid[k], target_lower[k]))
        def _():
            ring[k].start()

    loads[2].wait()
    loads[4].wait()
    loads[5].wait()
    mine = quarter_ref[lax.rem(me, 4)]

    def columns(which):
        lines = recv[pl.ds(8 * which, 8)]
        lines = [lines[:, c].reshape(64, 128) for c in range(5)]
        v, pressure, heat = physical(lines)
        fields = [f * mine[0:1] for f in flux(lines, v, pressure, 1)]
        viscous = [u * mine[1:2] for u in v] + [heat * mine[2:3]]
        shifts = [fields[0]] + [
            pltpu.roll(fields[0], 128 - 32 * g, 1) for g in range(1, 4)
        ]
        wide = jnp.concatenate(
            [
                jnp.concatenate(block_transpose(fields[1:], lane), axis=0),
                jnp.concatenate(shifts, axis=0),
            ],
            axis=1,
        )
        thin = jnp.concatenate(block_transpose(viscous, lane), axis=0)
        return split(wide), split(thin)

    def product(rows, which, inputs):
        parts = []
        for order, (x_high, x_low) in enumerate(inputs):
            a_high = high[rows, which, order]
            a_low = low[rows, which, order]

            def dot(a, b):
                return jnp.dot(a, b, preferred_element_type=F32)

            parts.append(
                dot(a_high, x_high) + (dot(a_high, x_low) + dot(a_low, x_high))
            )
        wide, thin = parts
        return wide[:, :128] + thin, wide[:, 128:]

    def deliver(rows, main, edge):
        main = [main[64 * g : 64 * g + 64] for g in range(4)]
        edge = [edge[64 * g : 64 * g + 64] for g in range(4)]
        plain = edge[0]
        for g in range(1, 4):
            plain = jnp.where(
                lane // 32 == g, pltpu.roll(edge[g], 32 * g, 1), plain
            )
        for c, value in enumerate((plain,) + tuple(block_transpose(main, lane))):
            send[pl.ds(8 * rows, 8), c] = value.reshape(8, 8, 128)

    for _, at in near_peers:
        pack_from(at).wait_recv()
    inputs = columns(half)
    far_main, far_edge = product(1 - half, half, inputs)
    near_main, near_edge = product(half, half, inputs)
    for _, at in far_peers:
        pack_from(at).wait_recv()
    inputs = columns(1 - half)
    main, edge = product(1 - half, 1 - half, inputs)
    deliver(1 - half, far_main + main, far_edge + edge)
    for peer, at in far_peers:
        back_copy(peer, at).start()
    main, edge = product(half, 1 - half, inputs)
    deliver(half, near_main + main, near_edge + edge)
    for peer, at in near_peers:
        back_copy(peer, at).start()
    back[me] = send[me]

    for k in range(2):

        @pl.when(both(valid[k], jnp.logical_not(target_lower[k])))
        def _():
            pl.semaphore_wait(ring_ready.at[k], 1)
            ring[k].start()

    @pl.when(plane_at == 0)
    def _():
        pl.semaphore_wait(halo_ready.at[1], 1)
        to_left.start()

    ring[0].wait_recv()

    @pl.when(valid[1])
    def _():
        ring[1].wait_recv()

    @pl.when(jnp.logical_not(valid[1]))
    def _():
        pairs[2] = pairs[0]

    totals[me] = pairs[1] + pairs[2]
    for peer, at in ordered:
        total_copy(peer, at).start()

    to_right.wait_recv()
    to_left.wait_recv()
    planes_flux, planes_visc = [], []
    for block in (halo.at[0], q_ref, halo.at[1]):
        cells = [block[c].reshape(128, 128) for c in range(5)]
        v, pressure, heat = physical(cells)
        fields = [f.reshape(4, 32, 128) for f in flux(cells, v, pressure, 0)]
        others = [f.reshape(4, 32, 128) for f in v + [heat]]
        for plane in range(4):
            planes_flux.append([f[plane] for f in fields])
            planes_visc.append([f[plane] for f in others])
    for plane in range(4):
        at = plane + 4
        for c in range(5):
            value = out_ref[c, plane]
            for k in range(1, 5):
                weight = -TIME_STEP * FIRST_COEFFS[k - 1] / AXIAL_STEP
                value = value + weight * (
                    planes_flux[at + k][c] - planes_flux[at - k][c]
                )
            if c:
                factor = (CONDUCTION if c == 4 else VISCOSITY) * TIME_STEP
                factor = factor / (AXIAL_STEP * AXIAL_STEP)
                value = value + factor * SECOND_CENTER * planes_visc[at][c - 1]
                for k in range(1, 5):
                    value = value + factor * SECOND_COEFFS[k - 1] * (
                        planes_visc[at + k][c - 1] + planes_visc[at - k][c - 1]
                    )
            out_ref[c, plane] = value

    for _, at in near_peers + far_peers:
        back_from(at).wait_recv()
    for _, at in ordered:
        total_from(at).wait_recv()
    total = totals[0]
    for s in range(1, NSEC):
        total = total + totals[s]
    bulk = jnp.sum(total, axis=1, keepdims=True) * scale
    forcing = (TIME_STEP * FORCE_RATE) * (TARGET_BULK - bulk)
    ret = [
        jnp.stack([back[4 * p + quarter] for p in range(4)]).reshape(160, 128)
        for quarter in range(4)
    ]
    for g, value in enumerate(block_transpose(ret, lane)):
        value = value.reshape(4, 5, 8, 128)
        rows = slice(8 * g, 8 * g + 8)
        for c in range(5):
            more = value[:, c]
            if c == 1:
                more = more + forcing.reshape(1, 1, 1)
            if c == 4:
                more = more + forcing.reshape(1, 1, 1) * (
                    q_ref[1, :, rows, :] / q_ref[0, :, rows, :]
                )
            out_ref[c, :, rows, :] = out_ref[c, :, rows, :] + more

    for peer, at in ordered:
        sums_copy(peer, at).wait_send()
        pack_copy(peer, at).wait_send()
        back_copy(peer, at).wait_send()
        total_copy(peer, at).wait_send()
    to_right.wait_send()
    to_left.wait_send()
    ring[0].wait_send()

    @pl.when(valid[1])
    def _():
        ring[1].wait_send()


def solution(mesh):
    high, low, radial, rows, quarter, scale = constants()

    def shards(balance_quantities, register):
        vmem = pl.BlockSpec(memory_space=pltpu.VMEM)
        hbm = pl.BlockSpec(memory_space=pltpu.HBM)
        dma = pltpu.SemaphoreType.DMA
        chunk = pltpu.VMEM((NSEC, 5, 8, 128), F32)
        line = pltpu.VMEM((NSEC, 1, 128), F32)
        each = dma((NSEC,))
        operands = (balance_quantities, high, low, radial, rows, quarter)
        tendency = pl.pallas_call(
            functools.partial(body, scale),
            out_shape=jax.ShapeDtypeStruct((5, 4, 32, R), F32),
            in_specs=[hbm] * 6,
            out_specs=vmem,
            scratch_shapes=[pltpu.VMEM(o.shape, o.dtype) for o in operands]
            + [chunk] * 4
            + [
                pltpu.VMEM((2, 5, 4, 32, R), F32),
                line,
                pltpu.VMEM((3, 1, 128), F32),
                line,
                dma((6,)),
                each,
                each,
                each,
                each,
                dma((2,)),
                dma((2,)),
                each,
                each,
                each,
                each,
                dma((2,)),
                dma((2,)),
                pltpu.SemaphoreType.REGULAR((2,)),
                pltpu.SemaphoreType.REGULAR((2,)),
            ],
            compiler_params=pltpu.CompilerParams(
                collective_id=0,
                has_side_effects=True,
                vmem_limit_bytes=60 * 1024 * 1024,
            ),
        )(*operands)
        register_new = SECTION_DECAY * register + tendency
        conserved_new = balance_quantities + SEGMENT_WEIGHT * register_new
        return conserved_new, register_new

    spec = P(None, "ax", "sec", None)
    return jax.shard_map(
        shards,
        mesh=mesh,
        in_specs=(spec, spec),
        out_specs=(spec, spec),
        check_vma=False,
    )
```

```python
import functools

import jax
import jax.numpy as jnp
import ml_dtypes
import numpy as np
from jax import lax
from jax.experimental import pallas as pl
from jax.experimental.pallas import tpu as pltpu
from jax.sharding import PartitionSpec as P

AXIAL_STEP = 0.003
TIME_STEP = 0.001
SECTION_DECAY = -5.0 / 9.0
SEGMENT_WEIGHT = 15.0 / 16.0
VISCOSITY = 2.5e-05
CONDUCTION = VISCOSITY / (0.4 * 0.7)
TARGET_BULK = 0.4
FORCE_RATE = 8000.0
FIRST_COEFFS = (4.0 / 5.0, -1.0 / 5.0, 4.0 / 105.0, -1.0 / 280.0)
SECOND_CENTER = -205.0 / 72.0
SECOND_COEFFS = (8.0 / 5.0, -1.0 / 5.0, 8.0 / 315.0, -1.0 / 560.0)
HIGHEST = lax.Precision.HIGHEST
MESH = pl.DeviceIdType.MESH

R = 128
NTH = 512
NZ = 128
NSEC = 16
NAX = 32
F32 = jnp.float32
BF16 = jnp.bfloat16


def constants():
    index = np.arange(R)
    nodes = np.cos(np.pi * index / (R - 1))
    radius = 0.625 + 0.375 * nodes
    ends = np.where((index == 0) | (index == R - 1), 2.0, 1.0)
    spread = nodes[:, None] - nodes[None, :]
    np.fill_diagonal(spread, 1.0)
    parity = np.where((index[:, None] + index[None, :]) % 2 == 0, 1.0, -1.0)
    off = ends[:, None] / ends[None, :] * parity / spread
    np.fill_diagonal(off, 0.0)
    first = (off - np.diag(off.sum(axis=1))) * (2.0 / 0.75)
    second = first @ first

    lag = (np.arange(NTH)[:, None] - np.arange(NTH)[None, :]) % NTH
    step = 2.0 * np.pi / NTH
    sign = np.where(lag % 2 == 0, 1.0, -1.0)
    safe = np.where(lag == 0, 1, lag)
    azim_first = np.where(lag == 0, 0.0, 0.5 * sign / np.tan(safe * step / 2))
    azim_second = np.where(
        lag == 0,
        -np.pi * np.pi / (3.0 * step * step) - 1.0 / 6.0,
        -0.5 * sign / np.sin(safe * step / 2) ** 2,
    )
    order = np.arange(NTH).reshape(4, 2, 2, 4, 8).transpose(1, 3, 0, 2, 4).reshape(NTH)
    both = np.stack([azim_first[order][:, order], azim_second[order][:, order]])
    both = both.reshape(2, 2, 256, 2, 256).transpose(1, 3, 0, 2, 4)
    both = both.astype(np.float32)
    high = both.astype(ml_dtypes.bfloat16)
    low = (both - high.astype(np.float32)).astype(ml_dtypes.bfloat16)

    flux_op = -TIME_STEP * (first * radius[None, :]) / radius[:, None]
    diff_op = TIME_STEP * (second + first / radius[:, None])
    radial = np.stack(
        [flux_op.T, VISCOSITY * diff_op.T, CONDUCTION * diff_op.T]
    ).astype(np.float32)

    rows = np.zeros((8, R), np.float32)
    rows[0] = radius
    rows[1] = 1.0 / radius
    quarter = np.zeros((4, 8, R), np.float32)
    for q in range(4):
        own = np.tile(radius[32 * q : 32 * q + 32], 4)
        quarter[q, 0] = -TIME_STEP / own
        quarter[q, 1] = TIME_STEP * VISCOSITY / own**2
        quarter[q, 2] = TIME_STEP * CONDUCTION / own**2
    scale = 1.0 / (NZ * NTH * radius.sum())
    return high, low, radial, rows, quarter, float(scale)


def block_transpose(v, lane):
    v0, v1, v2, v3 = v
    low = lane < 64
    even = (lane // 32) % 2 == 0

    def swap(a, b, mask, shift):
        return (
            jnp.where(mask, a, pltpu.roll(b, shift, 1)),
            jnp.where(mask, pltpu.roll(a, 128 - shift, 1), b),
        )

    a0, a2 = swap(v0, v2, low, 64)
    a1, a3 = swap(v1, v3, low, 64)
    b0, b1 = swap(a0, a1, even, 32)
    b2, b3 = swap(a2, a3, even, 32)
    return b0, b1, b2, b3


def physical(q):
    inverse = 1.0 / q[0]
    v = [q[1] * inverse, q[2] * inverse, q[3] * inverse]
    pressure = 0.4 * (q[4] - 0.5 * (q[1] * v[0] + q[2] * v[1] + q[3] * v[2]))
    return v, pressure, pressure * inverse


def flux(q, v, pressure, direction):
    w = v[direction]
    out = [q[1 + direction], q[1] * w, q[2] * w, q[3] * w, (q[4] + pressure) * w]
    out[1 + direction] = out[1 + direction] + pressure
    return out


def split(x):
    high = x.astype(BF16)
    return high, (x - high.astype(F32)).astype(BF16)


def body(
    scale,
    q_hbm,
    high_hbm,
    low_hbm,
    radial_hbm,
    rows_hbm,
    quarter_hbm,
    out_ref,
    q_ref,
    high,
    low,
    radial_ref,
    rows_ref,
    quarter_ref,
    pack,
    recv,
    send,
    back,
    halo,
    sums,
    slabs,
    load_sem,
    a_send,
    a_recv,
    s_send,
    s_recv,
    b_send,
    b_recv,
    t_send,
    t_recv,
    h_send,
    h_recv,
    halo_ready,
    slab_ready,
):
    ax = lax.axis_index("ax")
    sec = lax.axis_index("sec")
    x, half, core = sec // 4, lax.rem(sec // 2, 2), lax.rem(sec, 2)
    me = 8 * half + 2 * x + core

    def remote(src, dst, send_sem, recv_sem, to_ax, to_sec):
        return pltpu.make_async_remote_copy(
            src_ref=src,
            dst_ref=dst,
            send_sem=send_sem,
            recv_sem=recv_sem,
            device_id=(to_ax, to_sec),
            device_id_type=MESH,
        )

    def at_sector(to_x, to_half, to_core):
        return 4 * to_x + 2 * to_half + to_core, 8 * to_half + 2 * to_x + to_core

    def shifted(dx):
        return lax.rem(x + dx, 4)

    far_peers = [
        at_sector(shifted(dx), 1 - half, c) for c in range(2) for dx in (2, 1, 3, 0)
    ]
    near_peers = [
        at_sector(shifted(dx), half, c) for c in range(2) for dx in (2, 1, 3)
    ] + [at_sector(x, half, 1 - core)]
    ordered = far_peers[:4] + near_peers[:3] + far_peers[4:] + near_peers[3:]

    plane_at = lax.rem(ax, 8)
    right = lax.rem(ax + 1, NAX)
    left = lax.rem(ax + NAX - 1, NAX)

    def rank(at):
        return 4 * lax.rem(at, 8) + at // 8

    def ranked(at):
        return 8 * lax.rem(at, 4) + at // 4

    mine_rank = rank(ax)

    def each_rank(low, high, action):
        lax.fori_loop(low, high, lambda r, _: (action(ranked(r)), 0)[1], 0)

    def signal(sem, to_ax, to_sec):
        pl.semaphore_signal(
            sem, inc=1, device_id=(to_ax, to_sec), device_id_type=MESH
        )

    barrier = pltpu.get_barrier_semaphore()
    loads = [
        pltpu.make_async_copy(src, dst, load_sem.at[i])
        for i, (src, dst) in enumerate(
            (
                (q_hbm, q_ref),
                (rows_hbm, rows_ref),
                (quarter_hbm, quarter_ref),
                (radial_hbm, radial_ref),
                (high_hbm, high),
                (low_hbm, low),
            )
        )
    ]
    loads[0].start()
    loads[1].start()
    for peer, _ in ordered:
        signal(barrier, ax, peer)

    each_rank(mine_rank + 1, NAX, lambda to: signal(barrier, to, sec))
    for copy in loads[2:]:
        copy.start()

    loads[0].wait()
    loads[1].wait()
    radius = rows_ref[0:1, :]
    flow = jnp.sum(q_ref[1].reshape(128, 128) * radius, axis=0, keepdims=True)
    slabs[ax] = flow

    lane = lax.broadcasted_iota(jnp.int32, (1, 128), 1)
    groups = [
        q_ref[:, :, 8 * g : 8 * g + 8, :].reshape(160, 128) for g in range(4)
    ]
    for quarter, packed in enumerate(block_transpose(groups, lane)):
        packed = packed.reshape(5, 4, 8, 128)
        for plane in range(4):
            pack[4 * plane + quarter] = packed[:, plane]

    pl.semaphore_wait(barrier, 15 + mine_rank)

    def sums_copy(peer, at):
        return remote(sums.at[me], sums.at[me], s_send.at[at], s_recv.at[me], ax, peer)

    def sums_from(at):
        return remote(sums.at[at], sums.at[at], s_send.at[at], s_recv.at[at], ax, sec)

    def pack_copy(peer, at):
        return remote(pack.at[at], recv.at[me], a_send.at[at], a_recv.at[me], ax, peer)

    def pack_from(at):
        return remote(pack.at[at], recv.at[at], a_send.at[at], a_recv.at[at], ax, sec)

    def back_copy(peer, at):
        return remote(send.at[at], back.at[me], b_send.at[at], b_recv.at[me], ax, peer)

    def back_from(at):
        return remote(send.at[at], back.at[at], b_send.at[at], b_recv.at[at], ax, sec)

    def slab_copy(to):
        return remote(slabs.at[ax], slabs.at[ax], t_send.at[to], t_recv.at[ax], to, sec)

    def slab_from(to):
        return remote(slabs.at[to], slabs.at[to], t_send.at[to], t_recv.at[to], to, sec)

    to_right = remote(q_ref, halo.at[0], h_send.at[0], h_recv.at[0], right, sec)
    to_left = remote(q_ref, halo.at[1], h_send.at[1], h_recv.at[1], left, sec)
    each_rank(0, mine_rank, lambda to: slab_copy(to).start())

    for peer, at in ordered:
        pack_copy(peer, at).start()

    @pl.when(plane_at != 0)
    def _():
        signal(halo_ready.at[0], left, sec)

    @pl.when(plane_at == 7)
    def _():
        signal(halo_ready.at[1], right, sec)

    @pl.when(plane_at != 0)
    def _():
        to_left.start()

    each_rank(0, mine_rank, lambda to: signal(slab_ready, to, sec))
    recv[me] = pack[me]

    loads[3].wait()
    whole = [q_ref[c].reshape(128, 128) for c in range(5)]
    v, pressure, heat = physical(whole)
    inverse_radius = rows_ref[1:2, :]
    diffused = v + [heat]
    tend = []
    for c, field in enumerate(flux(whole, v, pressure, 2)):
        value = jnp.dot(
            field, radial_ref[0], precision=HIGHEST, preferred_element_type=F32
        )
        if c:
            value = value + jnp.dot(
                diffused[c - 1],
                radial_ref[2 if c == 4 else 1],
                precision=HIGHEST,
                preferred_element_type=F32,
            )
        tend.append(value)
    turn = TIME_STEP * inverse_radius
    tend[2] = tend[2] - whole[2] * v[2] * turn
    tend[3] = tend[3] + (whole[2] * v[1] + pressure) * turn
    for c in range(5):
        out_ref[c] = tend[c].reshape(4, 32, 128)

    @pl.when(plane_at != 7)
    def _():
        pl.semaphore_wait(halo_ready.at[0], 1)
        to_right.start()

    loads[2].wait()
    loads[4].wait()
    loads[5].wait()
    mine = quarter_ref[lax.rem(me, 4)]

    def columns(which):
        lines = recv[pl.ds(8 * which, 8)]
        lines = [lines[:, c].reshape(64, 128) for c in range(5)]
        v, pressure, heat = physical(lines)
        fields = [f * mine[0:1] for f in flux(lines, v, pressure, 1)]
        viscous = [u * mine[1:2] for u in v] + [heat * mine[2:3]]
        shifts = [fields[0]] + [
            pltpu.roll(fields[0], 128 - 32 * g, 1) for g in range(1, 4)
        ]
        wide = jnp.concatenate(
            [
                jnp.concatenate(block_transpose(fields[1:], lane), axis=0),
                jnp.concatenate(shifts, axis=0),
            ],
            axis=1,
        )
        thin = jnp.concatenate(block_transpose(viscous, lane), axis=0)
        return split(wide), split(thin)

    def product(rows, which, inputs):
        parts = []
        for order, (x_high, x_low) in enumerate(inputs):
            a_high = high[rows, which, order]
            a_low = low[rows, which, order]

            def dot(a, b):
                return jnp.dot(a, b, preferred_element_type=F32)

            parts.append(
                dot(a_high, x_high) + (dot(a_high, x_low) + dot(a_low, x_high))
            )
        wide, thin = parts
        return wide[:, :128] + thin, wide[:, 128:]

    def deliver(rows, main, edge):
        main = [main[64 * g : 64 * g + 64] for g in range(4)]
        edge = [edge[64 * g : 64 * g + 64] for g in range(4)]
        plain = edge[0]
        for g in range(1, 4):
            plain = jnp.where(
                lane // 32 == g, pltpu.roll(edge[g], 32 * g, 1), plain
            )
        for c, value in enumerate((plain,) + tuple(block_transpose(main, lane))):
            send[pl.ds(8 * rows, 8), c] = value.reshape(8, 8, 128)

    for _, at in near_peers:
        pack_from(at).wait_recv()
    inputs = columns(half)
    far_main, far_edge = product(1 - half, half, inputs)
    near_main, near_edge = product(half, half, inputs)

    @pl.when(mine_rank < NAX - 1)
    def _():
        pl.semaphore_wait(slab_ready, NAX - 1 - mine_rank)

    each_rank(mine_rank + 1, NAX, lambda to: slab_copy(to).start())
    for peer, at in ordered:
        pack_copy(peer, at).wait_send()

    @pl.when(plane_at == 7)
    def _():
        to_right.start()

    for _, at in far_peers:
        pack_from(at).wait_recv()
    inputs = columns(1 - half)
    main, edge = product(1 - half, 1 - half, inputs)
    deliver(1 - half, far_main + main, far_edge + edge)

    @pl.when(plane_at == 7)
    def _():
        to_right.wait_send()

    for peer, at in far_peers:
        back_copy(peer, at).start()
    main, edge = product(half, 1 - half, inputs)
    deliver(half, near_main + main, near_edge + edge)
    for peer, at in near_peers:
        back_copy(peer, at).start()
    back[me] = send[me]

    each_rank(0, mine_rank, lambda to: slab_from(to).wait_recv())
    each_rank(mine_rank + 1, NAX, lambda to: slab_from(to).wait_recv())
    total = slabs[0]
    for s in range(1, NAX):
        total = total + slabs[s]
    sums[me] = total
    for peer, at in ordered:
        sums_copy(peer, at).start()
    for peer, at in ordered:
        back_copy(peer, at).wait_send()

    @pl.when(plane_at == 0)
    def _():
        pl.semaphore_wait(halo_ready.at[1], 1)
        to_left.start()

    to_right.wait_recv()
    to_left.wait_recv()
    planes_flux, planes_visc = [], []
    for block in (halo.at[0], q_ref, halo.at[1]):
        cells = [block[c].reshape(128, 128) for c in range(5)]
        v, pressure, heat = physical(cells)
        fields = [f.reshape(4, 32, 128) for f in flux(cells, v, pressure, 0)]
        others = [f.reshape(4, 32, 128) for f in v + [heat]]
        for plane in range(4):
            planes_flux.append([f[plane] for f in fields])
            planes_visc.append([f[plane] for f in others])
    for plane in range(4):
        at = plane + 4
        for c in range(5):
            value = out_ref[c, plane]
            for k in range(1, 5):
                weight = -TIME_STEP * FIRST_COEFFS[k - 1] / AXIAL_STEP
                value = value + weight * (
                    planes_flux[at + k][c] - planes_flux[at - k][c]
                )
            if c:
                factor = (CONDUCTION if c == 4 else VISCOSITY) * TIME_STEP
                factor = factor / (AXIAL_STEP * AXIAL_STEP)
                value = value + factor * SECOND_CENTER * planes_visc[at][c - 1]
                for k in range(1, 5):
                    value = value + factor * SECOND_COEFFS[k - 1] * (
                        planes_visc[at + k][c - 1] + planes_visc[at - k][c - 1]
                    )
            out_ref[c, plane] = value

    for _, at in near_peers + far_peers:
        back_from(at).wait_recv()
    for _, at in ordered:
        sums_from(at).wait_recv()
    total = sums[0]
    for s in range(1, NSEC):
        total = total + sums[s]
    bulk = jnp.sum(total, axis=1, keepdims=True) * scale
    forcing = (TIME_STEP * FORCE_RATE) * (TARGET_BULK - bulk)
    ret = [
        jnp.stack([back[4 * p + quarter] for p in range(4)]).reshape(160, 128)
        for quarter in range(4)
    ]
    for g, value in enumerate(block_transpose(ret, lane)):
        value = value.reshape(4, 5, 8, 128)
        rows = slice(8 * g, 8 * g + 8)
        for c in range(5):
            more = value[:, c]
            if c == 1:
                more = more + forcing.reshape(1, 1, 1)
            if c == 4:
                more = more + forcing.reshape(1, 1, 1) * (
                    q_ref[1, :, rows, :] / q_ref[0, :, rows, :]
                )
            out_ref[c, :, rows, :] = out_ref[c, :, rows, :] + more

    for peer, at in ordered:
        sums_copy(peer, at).wait_send()

    @pl.when(plane_at != 7)
    def _():
        to_right.wait_send()

    to_left.wait_send()
    each_rank(0, mine_rank, lambda to: slab_copy(to).wait_send())
    each_rank(mine_rank + 1, NAX, lambda to: slab_copy(to).wait_send())


def solution(mesh):
    high, low, radial, rows, quarter, scale = constants()

    def shards(balance_quantities, register):
        vmem = pl.BlockSpec(memory_space=pltpu.VMEM)
        hbm = pl.BlockSpec(memory_space=pltpu.HBM)
        dma = pltpu.SemaphoreType.DMA
        chunk = pltpu.VMEM((NSEC, 5, 8, 128), F32)
        each = dma((NSEC,))
        operands = (balance_quantities, high, low, radial, rows, quarter)
        tendency = pl.pallas_call(
            functools.partial(body, scale),
            out_shape=jax.ShapeDtypeStruct((5, 4, 32, R), F32),
            in_specs=[hbm] * 6,
            out_specs=vmem,
            scratch_shapes=[pltpu.VMEM(o.shape, o.dtype) for o in operands]
            + [chunk] * 4
            + [
                pltpu.VMEM((2, 5, 4, 32, R), F32),
                pltpu.VMEM((NSEC, 1, 128), F32),
                pltpu.VMEM((NAX, 1, 128), F32),
                dma((6,)),
                each,
                each,
                each,
                each,
                each,
                each,
                dma((NAX,)),
                dma((NAX,)),
                dma((2,)),
                dma((2,)),
                pltpu.SemaphoreType.REGULAR((2,)),
                pltpu.SemaphoreType.REGULAR,
            ],
            compiler_params=pltpu.CompilerParams(
                collective_id=0,
                has_side_effects=True,
                vmem_limit_bytes=60 * 1024 * 1024,
            ),
        )(*operands)
        register_new = SECTION_DECAY * register + tendency
        conserved_new = balance_quantities + SEGMENT_WEIGHT * register_new
        return conserved_new, register_new

    spec = P(None, "ax", "sec", None)
    return jax.shard_map(
        shards,
        mesh=mesh,
        in_specs=(spec, spec),
        out_specs=(spec, spec),
        check_vma=False,
    )
```

```python
import functools

import jax
import jax.numpy as jnp
import ml_dtypes
import numpy as np
from jax import lax
from jax.experimental import pallas as pl
from jax.experimental.pallas import tpu as pltpu
from jax.sharding import PartitionSpec as P

AXIAL_STEP = 0.003
TIME_STEP = 0.001
SECTION_DECAY = -5.0 / 9.0
SEGMENT_WEIGHT = 15.0 / 16.0
VISCOSITY = 2.5e-05
CONDUCTION = VISCOSITY / (0.4 * 0.7)
TARGET_BULK = 0.4
FORCE_RATE = 8000.0
FIRST_COEFFS = (4.0 / 5.0, -1.0 / 5.0, 4.0 / 105.0, -1.0 / 280.0)
SECOND_CENTER = -205.0 / 72.0
SECOND_COEFFS = (8.0 / 5.0, -1.0 / 5.0, 8.0 / 315.0, -1.0 / 560.0)
HIGHEST = lax.Precision.HIGHEST
MESH = pl.DeviceIdType.MESH

R = 128
NTH = 512
NZ = 128
NSEC = 16
NAX = 32
F32 = jnp.float32
BF16 = jnp.bfloat16


def constants():
    index = np.arange(R)
    nodes = np.cos(np.pi * index / (R - 1))
    radius = 0.625 + 0.375 * nodes
    ends = np.where((index == 0) | (index == R - 1), 2.0, 1.0)
    spread = nodes[:, None] - nodes[None, :]
    np.fill_diagonal(spread, 1.0)
    parity = np.where((index[:, None] + index[None, :]) % 2 == 0, 1.0, -1.0)
    off = ends[:, None] / ends[None, :] * parity / spread
    np.fill_diagonal(off, 0.0)
    first = (off - np.diag(off.sum(axis=1))) * (2.0 / 0.75)
    second = first @ first

    lag = (np.arange(NTH)[:, None] - np.arange(NTH)[None, :]) % NTH
    step = 2.0 * np.pi / NTH
    sign = np.where(lag % 2 == 0, 1.0, -1.0)
    safe = np.where(lag == 0, 1, lag)
    azim_first = np.where(lag == 0, 0.0, 0.5 * sign / np.tan(safe * step / 2))
    azim_second = np.where(
        lag == 0,
        -np.pi * np.pi / (3.0 * step * step) - 1.0 / 6.0,
        -0.5 * sign / np.sin(safe * step / 2) ** 2,
    )
    order = np.arange(NTH).reshape(4, 2, 2, 4, 8).transpose(1, 3, 0, 2, 4).reshape(NTH)
    both = np.stack([azim_first[order][:, order], azim_second[order][:, order]])
    both = both.reshape(2, 2, 256, 2, 256).transpose(1, 3, 0, 2, 4)
    both = both.astype(np.float32)
    high = both.astype(ml_dtypes.bfloat16)
    low = (both - high.astype(np.float32)).astype(ml_dtypes.bfloat16)

    flux_op = -TIME_STEP * (first * radius[None, :]) / radius[:, None]
    diff_op = TIME_STEP * (second + first / radius[:, None])
    radial = np.stack(
        [flux_op.T, VISCOSITY * diff_op.T, CONDUCTION * diff_op.T]
    ).astype(np.float32)

    rows = np.zeros((8, R), np.float32)
    rows[0] = radius
    rows[1] = 1.0 / radius
    quarter = np.zeros((4, 8, R), np.float32)
    for q in range(4):
        own = np.tile(radius[32 * q : 32 * q + 32], 4)
        quarter[q, 0] = -TIME_STEP / own
        quarter[q, 1] = TIME_STEP * VISCOSITY / own**2
        quarter[q, 2] = TIME_STEP * CONDUCTION / own**2
    scale = 1.0 / (NZ * NTH * radius.sum())
    return high, low, radial, rows, quarter, float(scale)


def block_transpose(v, lane):
    v0, v1, v2, v3 = v
    low = lane < 64
    even = (lane // 32) % 2 == 0

    def swap(a, b, mask, shift):
        return (
            jnp.where(mask, a, pltpu.roll(b, shift, 1)),
            jnp.where(mask, pltpu.roll(a, 128 - shift, 1), b),
        )

    a0, a2 = swap(v0, v2, low, 64)
    a1, a3 = swap(v1, v3, low, 64)
    b0, b1 = swap(a0, a1, even, 32)
    b2, b3 = swap(a2, a3, even, 32)
    return b0, b1, b2, b3


def physical(q):
    inverse = 1.0 / q[0]
    v = [q[1] * inverse, q[2] * inverse, q[3] * inverse]
    pressure = 0.4 * (q[4] - 0.5 * (q[1] * v[0] + q[2] * v[1] + q[3] * v[2]))
    return v, pressure, pressure * inverse


def flux(q, v, pressure, direction):
    w = v[direction]
    out = [q[1 + direction], q[1] * w, q[2] * w, q[3] * w, (q[4] + pressure) * w]
    out[1 + direction] = out[1 + direction] + pressure
    return out


def split(x):
    high = x.astype(BF16)
    return high, (x - high.astype(F32)).astype(BF16)


def body(
    scale,
    q_hbm,
    high_hbm,
    low_hbm,
    radial_hbm,
    rows_hbm,
    quarter_hbm,
    out_ref,
    q_ref,
    high,
    low,
    radial_ref,
    rows_ref,
    quarter_ref,
    pack,
    recv,
    send,
    back,
    halo,
    relay,
    sums,
    slabs,
    load_sem,
    a_send,
    a_recv,
    s_send,
    s_recv,
    b_send,
    b_recv,
    t_send,
    t_recv,
    p_send,
    h_send,
    h_recv,
    r_send,
    r_recv,
    f_send,
    halo_ready,
    slab_ready,
):
    ax = lax.axis_index("ax")
    sec = lax.axis_index("sec")
    x, half, core = sec // 4, lax.rem(sec // 2, 2), lax.rem(sec, 2)
    me = 8 * half + 2 * x + core

    def remote(src, dst, send_sem, recv_sem, to_ax, to_sec):
        return pltpu.make_async_remote_copy(
            src_ref=src,
            dst_ref=dst,
            send_sem=send_sem,
            recv_sem=recv_sem,
            device_id=(to_ax, to_sec),
            device_id_type=MESH,
        )

    def at_sector(to_x, to_half, to_core):
        return 4 * to_x + 2 * to_half + to_core, 8 * to_half + 2 * to_x + to_core

    def shifted(dx):
        return lax.rem(x + dx, 4)

    far_peers = [
        at_sector(shifted(dx), 1 - half, c) for c in range(2) for dx in (2, 1, 3, 0)
    ]
    near_peers = [
        at_sector(shifted(dx), half, c) for c in range(2) for dx in (2, 1, 3)
    ] + [at_sector(x, half, 1 - core)]
    ordered = far_peers[:4] + near_peers[:3] + far_peers[4:] + near_peers[3:]

    plane_at = lax.rem(ax, 8)
    right = lax.rem(ax + 1, NAX)
    left = lax.rem(ax + NAX - 1, NAX)

    def rank(at):
        return 4 * lax.rem(at, 8) + at // 8

    def ranked(at):
        return 8 * lax.rem(at, 4) + at // 4

    mine_rank = rank(ax)

    def each_rank(low, high, action):
        lax.fori_loop(low, high, lambda r, _: (action(ranked(r)), 0)[1], 0)

    def signal(sem, to_ax, to_sec):
        pl.semaphore_signal(
            sem, inc=1, device_id=(to_ax, to_sec), device_id_type=MESH
        )

    barrier = pltpu.get_barrier_semaphore()
    loads = [
        pltpu.make_async_copy(src, dst, load_sem.at[i])
        for i, (src, dst) in enumerate(
            (
                (q_hbm, q_ref),
                (rows_hbm, rows_ref),
                (quarter_hbm, quarter_ref),
                (radial_hbm, radial_ref),
                (high_hbm, high),
                (low_hbm, low),
            )
        )
    ]
    loads[0].start()
    loads[1].start()
    for peer, _ in ordered:
        signal(barrier, ax, peer)

    each_rank(mine_rank + 1, NAX, lambda to: signal(barrier, to, sec))
    for copy in loads[2:]:
        copy.start()

    loads[0].wait()
    loads[1].wait()
    radius = rows_ref[0:1, :]
    flow = jnp.sum(q_ref[1].reshape(128, 128) * radius, axis=0, keepdims=True)
    slabs[ax] = flow

    lane = lax.broadcasted_iota(jnp.int32, (1, 128), 1)
    groups = [
        q_ref[:, :, 8 * g : 8 * g + 8, :].reshape(160, 128) for g in range(4)
    ]
    for quarter, packed in enumerate(block_transpose(groups, lane)):
        packed = packed.reshape(5, 4, 8, 128)
        for plane in range(4):
            pack[4 * plane + quarter] = packed[:, plane]

    pl.semaphore_wait(barrier, 15 + mine_rank)
    each_rank(0, mine_rank, lambda to: signal(slab_ready, to, sec))

    @pl.when(plane_at == 7)
    def _():
        signal(halo_ready.at[1], right, sec)

    def sums_copy(peer, at):
        return remote(sums.at[me], sums.at[me], s_send.at[at], s_recv.at[me], ax, peer)

    def sums_from(at):
        return remote(sums.at[at], sums.at[at], s_send.at[at], s_recv.at[at], ax, sec)

    def pack_copy(peer, at):
        return remote(pack.at[at], recv.at[me], a_send.at[at], a_recv.at[me], ax, peer)

    def pack_from(at):
        return remote(pack.at[at], recv.at[at], a_send.at[at], a_recv.at[at], ax, sec)

    def back_copy(peer, at):
        return remote(send.at[at], back.at[me], b_send.at[at], b_recv.at[me], ax, peer)

    def back_from(at):
        return remote(send.at[at], back.at[at], b_send.at[at], b_recv.at[at], ax, sec)

    def slab_copy(to):
        return remote(slabs.at[ax], slabs.at[ax], t_send.at[to], t_recv.at[ax], to, sec)

    def proxy_copy(to):
        return remote(
            slabs.at[left], slabs.at[left], p_send.at[to], t_recv.at[left], to, sec
        )

    def slab_from(to):
        return remote(slabs.at[to], slabs.at[to], t_send.at[to], t_recv.at[to], to, sec)

    to_right = remote(q_ref, halo.at[0], h_send.at[0], h_recv.at[0], right, sec)
    to_left = remote(q_ref, halo.at[1], h_send.at[1], h_recv.at[1], left, sec)
    second_core = core == 1
    pass_on = remote(q_ref, relay, r_send, r_recv, right, sec)
    carry = remote(q_ref, relay, r_send, r_recv, lax.rem(ax + NAX - 7, NAX), sec)
    forward_right = remote(
        relay, halo.at[0], f_send, h_recv.at[0], lax.rem(ax + 8, NAX), sec
    )
    forward_left = remote(
        relay, halo.at[1], f_send, h_recv.at[1], lax.rem(ax + NAX - 2, NAX), sec
    )

    def at_plane(where, which):
        return jnp.logical_and(plane_at == where, which)

    each_rank(0, mine_rank, lambda to: slab_copy(to).start())

    for peer, at in ordered:
        pack_copy(peer, at).start()

    @pl.when(at_plane(7, second_core))
    def _():
        carry.start()

    @pl.when(plane_at != 0)
    def _():
        signal(halo_ready.at[0], left, sec)

    @pl.when(plane_at != 0)
    def _():
        to_left.start()

    recv[me] = pack[me]

    loads[3].wait()
    whole = [q_ref[c].reshape(128, 128) for c in range(5)]
    v, pressure, heat = physical(whole)
    inverse_radius = rows_ref[1:2, :]
    diffused = v + [heat]
    tend = []
    for c, field in enumerate(flux(whole, v, pressure, 2)):
        value = jnp.dot(
            field, radial_ref[0], precision=HIGHEST, preferred_element_type=F32
        )
        if c:
            value = value + jnp.dot(
                diffused[c - 1],
                radial_ref[2 if c == 4 else 1],
                precision=HIGHEST,
                preferred_element_type=F32,
            )
        tend.append(value)
    turn = TIME_STEP * inverse_radius
    tend[2] = tend[2] - whole[2] * v[2] * turn
    tend[3] = tend[3] + (whole[2] * v[1] + pressure) * turn
    for c in range(5):
        out_ref[c] = tend[c].reshape(4, 32, 128)

    @pl.when(plane_at != 7)
    def _():
        pl.semaphore_wait(halo_ready.at[0], 1)

    @pl.when(plane_at == 0)
    def _():
        slab_copy(right).start()

    @pl.when(plane_at != 7)
    def _():
        to_right.start()

    @pl.when(at_plane(0, second_core))
    def _():
        pass_on.start()

    loads[2].wait()
    loads[4].wait()
    loads[5].wait()
    mine = quarter_ref[lax.rem(me, 4)]

    def columns(which):
        lines = recv[pl.ds(8 * which, 8)]
        lines = [lines[:, c].reshape(64, 128) for c in range(5)]
        v, pressure, heat = physical(lines)
        fields = [f * mine[0:1] for f in flux(lines, v, pressure, 1)]
        viscous = [u * mine[1:2] for u in v] + [heat * mine[2:3]]
        shifts = [fields[0]] + [
            pltpu.roll(fields[0], 128 - 32 * g, 1) for g in range(1, 4)
        ]
        wide = jnp.concatenate(
            [
                jnp.concatenate(block_transpose(fields[1:], lane), axis=0),
                jnp.concatenate(shifts, axis=0),
            ],
            axis=1,
        )
        thin = jnp.concatenate(block_transpose(viscous, lane), axis=0)
        return split(wide), split(thin)

    def product(rows, which, inputs):
        parts = []
        for order, (x_high, x_low) in enumerate(inputs):
            a_high = high[rows, which, order]
            a_low = low[rows, which, order]

            def dot(a, b):
                return jnp.dot(a, b, preferred_element_type=F32)

            parts.append(
                dot(a_high, x_high) + (dot(a_high, x_low) + dot(a_low, x_high))
            )
        wide, thin = parts
        return wide[:, :128] + thin, wide[:, 128:]

    def deliver(rows, main, edge):
        main = [main[64 * g : 64 * g + 64] for g in range(4)]
        edge = [edge[64 * g : 64 * g + 64] for g in range(4)]
        plain = edge[0]
        for g in range(1, 4):
            plain = jnp.where(
                lane // 32 == g, pltpu.roll(edge[g], 32 * g, 1), plain
            )
        for c, value in enumerate((plain,) + tuple(block_transpose(main, lane))):
            send[pl.ds(8 * rows, 8), c] = value.reshape(8, 8, 128)

    for _, at in near_peers:
        pack_from(at).wait_recv()
    inputs = columns(half)
    far_main, far_edge = product(1 - half, half, inputs)
    near_main, near_edge = product(half, half, inputs)

    def slabs_to_later():
        pl.semaphore_wait(slab_ready, NAX - 1 - mine_rank)
        each_rank(mine_rank + 1, NAX, lambda to: slab_copy(to).start())

    @pl.when(plane_at == 1)
    def _():
        slab_from(left).wait_recv()
        each_rank(mine_rank - 3, mine_rank, lambda to: proxy_copy(to).start())

    @pl.when(jnp.logical_and(plane_at != 0, mine_rank < NAX - 1))
    def _():
        slabs_to_later()

    @pl.when(plane_at == 1)
    def _():
        each_rank(mine_rank + 1, NAX, lambda to: proxy_copy(to).start())

    for peer, at in ordered:
        pack_copy(peer, at).wait_send()

    @pl.when(at_plane(7, core == 0))
    def _():
        to_right.start()

    for _, at in far_peers:
        pack_from(at).wait_recv()
    inputs = columns(1 - half)
    main, edge = product(1 - half, 1 - half, inputs)
    deliver(1 - half, far_main + main, far_edge + edge)


    @pl.when(at_plane(7, core == 0))
    def _():
        to_right.wait_send()

    for peer, at in far_peers:
        back_copy(peer, at).start()
    main, edge = product(half, 1 - half, inputs)
    deliver(half, near_main + main, near_edge + edge)
    for peer, at in near_peers:
        back_copy(peer, at).start()
    back[me] = send[me]

    gap = jnp.where(plane_at == 1, 4, 0)
    each_rank(0, mine_rank - gap, lambda to: slab_from(to).wait_recv())
    each_rank(
        mine_rank + jnp.where(plane_at == 1, -3, 1),
        mine_rank,
        lambda to: slab_from(to).wait_recv(),
    )
    each_rank(mine_rank + 1, NAX, lambda to: slab_from(to).wait_recv())
    total = slabs[0]
    for s in range(1, NAX):
        total = total + slabs[s]
    sums[me] = total
    for peer, at in ordered:
        sums_copy(peer, at).start()

    @pl.when(at_plane(0, second_core))
    def _():
        carry.wait_recv()
        forward_right.start()

    for peer, at in ordered:
        back_copy(peer, at).wait_send()

    @pl.when(plane_at == 0)
    def _():
        pl.semaphore_wait(halo_ready.at[1], 1)

    @pl.when(at_plane(0, core == 0))
    def _():
        to_left.start()

    @pl.when(at_plane(1, second_core))
    def _():
        pass_on.wait_recv()
        forward_left.start()

    to_right.wait_recv()
    to_left.wait_recv()
    planes_flux, planes_visc = [], []
    for block in (halo.at[0], q_ref, halo.at[1]):
        cells = [block[c].reshape(128, 128) for c in range(5)]
        v, pressure, heat = physical(cells)
        fields = [f.reshape(4, 32, 128) for f in flux(cells, v, pressure, 0)]
        others = [f.reshape(4, 32, 128) for f in v + [heat]]
        for plane in range(4):
            planes_flux.append([f[plane] for f in fields])
            planes_visc.append([f[plane] for f in others])
    for plane in range(4):
        at = plane + 4
        for c in range(5):
            value = out_ref[c, plane]
            for k in range(1, 5):
                weight = -TIME_STEP * FIRST_COEFFS[k - 1] / AXIAL_STEP
                value = value + weight * (
                    planes_flux[at + k][c] - planes_flux[at - k][c]
                )
            if c:
                factor = (CONDUCTION if c == 4 else VISCOSITY) * TIME_STEP
                factor = factor / (AXIAL_STEP * AXIAL_STEP)
                value = value + factor * SECOND_CENTER * planes_visc[at][c - 1]
                for k in range(1, 5):
                    value = value + factor * SECOND_COEFFS[k - 1] * (
                        planes_visc[at + k][c - 1] + planes_visc[at - k][c - 1]
                    )
            out_ref[c, plane] = value

    for _, at in near_peers + far_peers:
        back_from(at).wait_recv()
    for _, at in ordered:
        sums_from(at).wait_recv()
    total = sums[0]
    for s in range(1, NSEC):
        total = total + sums[s]
    bulk = jnp.sum(total, axis=1, keepdims=True) * scale
    forcing = (TIME_STEP * FORCE_RATE) * (TARGET_BULK - bulk)
    ret = [
        jnp.stack([back[4 * p + quarter] for p in range(4)]).reshape(160, 128)
        for quarter in range(4)
    ]
    for g, value in enumerate(block_transpose(ret, lane)):
        value = value.reshape(4, 5, 8, 128)
        rows = slice(8 * g, 8 * g + 8)
        for c in range(5):
            more = value[:, c]
            if c == 1:
                more = more + forcing.reshape(1, 1, 1)
            if c == 4:
                more = more + forcing.reshape(1, 1, 1) * (
                    q_ref[1, :, rows, :] / q_ref[0, :, rows, :]
                )
            out_ref[c, :, rows, :] = out_ref[c, :, rows, :] + more

    for peer, at in ordered:
        sums_copy(peer, at).wait_send()

    @pl.when(plane_at != 7)
    def _():
        to_right.wait_send()


    @pl.when(jnp.logical_or(plane_at != 0, core == 0))
    def _():
        to_left.wait_send()

    @pl.when(at_plane(0, second_core))
    def _():
        pass_on.wait_send()

    @pl.when(at_plane(7, second_core))
    def _():
        carry.wait_send()

    @pl.when(at_plane(0, second_core))
    def _():
        forward_right.wait_send()

    @pl.when(at_plane(1, second_core))
    def _():
        forward_left.wait_send()

    each_rank(0, mine_rank, lambda to: slab_copy(to).wait_send())

    @pl.when(plane_at == 0)
    def _():
        pl.semaphore_wait(slab_ready, NAX - 1 - mine_rank)
        slab_copy(right).wait_send()

    @pl.when(plane_at != 0)
    def _():
        each_rank(mine_rank + 1, NAX, lambda to: slab_copy(to).wait_send())

    @pl.when(plane_at == 1)
    def _():
        each_rank(mine_rank - 3, mine_rank, lambda to: proxy_copy(to).wait_send())
        each_rank(mine_rank + 1, NAX, lambda to: proxy_copy(to).wait_send())


def solution(mesh):
    high, low, radial, rows, quarter, scale = constants()

    def shards(balance_quantities, register):
        vmem = pl.BlockSpec(memory_space=pltpu.VMEM)
        hbm = pl.BlockSpec(memory_space=pltpu.HBM)
        dma = pltpu.SemaphoreType.DMA
        chunk = pltpu.VMEM((NSEC, 5, 8, 128), F32)
        each = dma((NSEC,))
        operands = (balance_quantities, high, low, radial, rows, quarter)
        tendency = pl.pallas_call(
            functools.partial(body, scale),
            out_shape=jax.ShapeDtypeStruct((5, 4, 32, R), F32),
            in_specs=[hbm] * 6,
            out_specs=vmem,
            scratch_shapes=[pltpu.VMEM(o.shape, o.dtype) for o in operands]
            + [chunk] * 4
            + [
                pltpu.VMEM((2, 5, 4, 32, R), F32),
                pltpu.VMEM((5, 4, 32, R), F32),
                pltpu.VMEM((NSEC, 1, 128), F32),
                pltpu.VMEM((NAX, 1, 128), F32),
                dma((6,)),
                each,
                each,
                each,
                each,
                each,
                each,
                dma((NAX,)),
                dma((NAX,)),
                dma((NAX,)),
                dma((2,)),
                dma((2,)),
                dma,
                dma,
                dma,
                pltpu.SemaphoreType.REGULAR((2,)),
                pltpu.SemaphoreType.REGULAR,
            ],
            compiler_params=pltpu.CompilerParams(
                collective_id=0,
                has_side_effects=True,
                vmem_limit_bytes=60 * 1024 * 1024,
            ),
        )(*operands)
        register_new = SECTION_DECAY * register + tendency
        conserved_new = balance_quantities + SEGMENT_WEIGHT * register_new
        return conserved_new, register_new

    spec = P(None, "ax", "sec", None)
    return jax.shard_map(
        shards,
        mesh=mesh,
        in_specs=(spec, spec),
        out_specs=(spec, spec),
        check_vma=False,
    )
```

```python
import functools

import jax
import jax.numpy as jnp
import ml_dtypes
import numpy as np
from jax import lax
from jax.experimental import pallas as pl
from jax.experimental.pallas import tpu as pltpu
from jax.sharding import PartitionSpec as P

AXIAL_STEP = 0.003
TIME_STEP = 0.001
SECTION_DECAY = -5.0 / 9.0
SEGMENT_WEIGHT = 15.0 / 16.0
VISCOSITY = 2.5e-05
CONDUCTION = VISCOSITY / (0.4 * 0.7)
TARGET_BULK = 0.4
FORCE_RATE = 8000.0
FIRST_COEFFS = (4.0 / 5.0, -1.0 / 5.0, 4.0 / 105.0, -1.0 / 280.0)
SECOND_CENTER = -205.0 / 72.0
SECOND_COEFFS = (8.0 / 5.0, -1.0 / 5.0, 8.0 / 315.0, -1.0 / 560.0)
HIGHEST = lax.Precision.HIGHEST
MESH = pl.DeviceIdType.MESH

R = 128
NTH = 512
NZ = 128
NSEC = 16
NAX = 32
F32 = jnp.float32
BF16 = jnp.bfloat16


def constants():
    index = np.arange(R)
    nodes = np.cos(np.pi * index / (R - 1))
    radius = 0.625 + 0.375 * nodes
    ends = np.where((index == 0) | (index == R - 1), 2.0, 1.0)
    spread = nodes[:, None] - nodes[None, :]
    np.fill_diagonal(spread, 1.0)
    parity = np.where((index[:, None] + index[None, :]) % 2 == 0, 1.0, -1.0)
    off = ends[:, None] / ends[None, :] * parity / spread
    np.fill_diagonal(off, 0.0)
    first = (off - np.diag(off.sum(axis=1))) * (2.0 / 0.75)
    second = first @ first

    lag = (np.arange(NTH)[:, None] - np.arange(NTH)[None, :]) % NTH
    step = 2.0 * np.pi / NTH
    sign = np.where(lag % 2 == 0, 1.0, -1.0)
    safe = np.where(lag == 0, 1, lag)
    azim_first = np.where(lag == 0, 0.0, 0.5 * sign / np.tan(safe * step / 2))
    azim_second = np.where(
        lag == 0,
        -np.pi * np.pi / (3.0 * step * step) - 1.0 / 6.0,
        -0.5 * sign / np.sin(safe * step / 2) ** 2,
    )
    order = np.arange(NTH).reshape(4, 2, 2, 4, 8).transpose(1, 3, 0, 2, 4).reshape(NTH)
    both = np.stack([azim_first[order][:, order], azim_second[order][:, order]])
    both = both.reshape(2, 2, 256, 2, 256).transpose(1, 3, 0, 2, 4)
    both = both.astype(np.float32)
    high = both.astype(ml_dtypes.bfloat16)
    low = (both - high.astype(np.float32)).astype(ml_dtypes.bfloat16)

    flux_op = -TIME_STEP * (first * radius[None, :]) / radius[:, None]
    diff_op = TIME_STEP * (second + first / radius[:, None])
    radial = np.stack(
        [flux_op.T, VISCOSITY * diff_op.T, CONDUCTION * diff_op.T]
    ).astype(np.float32)

    rows = np.zeros((8, R), np.float32)
    rows[0] = radius
    rows[1] = 1.0 / radius
    quarter = np.zeros((4, 8, R), np.float32)
    for q in range(4):
        own = np.tile(radius[32 * q : 32 * q + 32], 4)
        quarter[q, 0] = -TIME_STEP / own
        quarter[q, 1] = TIME_STEP * VISCOSITY / own**2
        quarter[q, 2] = TIME_STEP * CONDUCTION / own**2
    scale = 1.0 / (NZ * NTH * radius.sum())
    return high, low, radial, rows, quarter, float(scale)


def block_transpose(v, lane):
    v0, v1, v2, v3 = v
    low = lane < 64
    even = (lane // 32) % 2 == 0

    def swap(a, b, mask, shift):
        return (
            jnp.where(mask, a, pltpu.roll(b, shift, 1)),
            jnp.where(mask, pltpu.roll(a, 128 - shift, 1), b),
        )

    a0, a2 = swap(v0, v2, low, 64)
    a1, a3 = swap(v1, v3, low, 64)
    b0, b1 = swap(a0, a1, even, 32)
    b2, b3 = swap(a2, a3, even, 32)
    return b0, b1, b2, b3


def physical(q):
    inverse = 1.0 / q[0]
    v = [q[1] * inverse, q[2] * inverse, q[3] * inverse]
    pressure = 0.4 * (q[4] - 0.5 * (q[1] * v[0] + q[2] * v[1] + q[3] * v[2]))
    return v, pressure, pressure * inverse


def flux(q, v, pressure, direction):
    w = v[direction]
    out = [q[1 + direction], q[1] * w, q[2] * w, q[3] * w, (q[4] + pressure) * w]
    out[1 + direction] = out[1 + direction] + pressure
    return out


def split(x):
    high = x.astype(BF16)
    return high, (x - high.astype(F32)).astype(BF16)


def body(
    scale,
    q_hbm,
    high_hbm,
    low_hbm,
    radial_hbm,
    rows_hbm,
    quarter_hbm,
    out_ref,
    q_ref,
    high,
    low,
    radial_ref,
    rows_ref,
    quarter_ref,
    pack,
    recv,
    send,
    back,
    halo,
    relay,
    sums,
    slabs,
    load_sem,
    a_send,
    a_recv,
    s_send,
    s_recv,
    b_send,
    b_recv,
    t_send,
    t_recv,
    p_send,
    h_send,
    h_recv,
    r_send,
    r_recv,
    f_send,
    halo_ready,
    slab_ready,
):
    ax = lax.axis_index("ax")
    sec = lax.axis_index("sec")
    x, half, core = sec // 4, lax.rem(sec // 2, 2), lax.rem(sec, 2)
    me = 8 * half + 2 * x + core

    def remote(src, dst, send_sem, recv_sem, to_ax, to_sec):
        return pltpu.make_async_remote_copy(
            src_ref=src,
            dst_ref=dst,
            send_sem=send_sem,
            recv_sem=recv_sem,
            device_id=(to_ax, to_sec),
            device_id_type=MESH,
        )

    def at_sector(to_x, to_half, to_core):
        return 4 * to_x + 2 * to_half + to_core, 8 * to_half + 2 * to_x + to_core

    def shifted(dx):
        return lax.rem(x + dx, 4)

    far_peers = [
        at_sector(shifted(dx), 1 - half, c) for c in range(2) for dx in (2, 1, 3, 0)
    ]
    near_peers = [
        at_sector(shifted(dx), half, c) for c in range(2) for dx in (2, 1, 3)
    ] + [at_sector(x, half, 1 - core)]
    ordered = far_peers + near_peers

    plane_at = lax.rem(ax, 8)
    right = lax.rem(ax + 1, NAX)
    left = lax.rem(ax + NAX - 1, NAX)

    def rank(at):
        return 4 * lax.rem(at, 8) + at // 8

    def ranked(at):
        return 8 * lax.rem(at, 4) + at // 4

    mine_rank = rank(ax)

    def each_rank(low, high, action):
        lax.fori_loop(low, high, lambda r, _: (action(ranked(r)), 0)[1], 0)

    def signal(sem, to_ax, to_sec):
        pl.semaphore_signal(
            sem, inc=1, device_id=(to_ax, to_sec), device_id_type=MESH
        )

    barrier = pltpu.get_barrier_semaphore()
    loads = [
        pltpu.make_async_copy(src, dst, load_sem.at[i])
        for i, (src, dst) in enumerate(
            (
                (q_hbm, q_ref),
                (rows_hbm, rows_ref),
                (quarter_hbm, quarter_ref),
                (radial_hbm, radial_ref),
                (high_hbm, high),
                (low_hbm, low),
            )
        )
    ]
    loads[0].start()
    loads[1].start()
    for peer, _ in ordered:
        signal(barrier, ax, peer)

    each_rank(mine_rank + 1, NAX, lambda to: signal(barrier, to, sec))
    for copy in loads[2:]:
        copy.start()

    loads[0].wait()
    loads[1].wait()
    radius = rows_ref[0:1, :]
    flow = jnp.sum(q_ref[1].reshape(128, 128) * radius, axis=0, keepdims=True)
    slabs[ax] = flow

    lane = lax.broadcasted_iota(jnp.int32, (1, 128), 1)
    groups = [
        q_ref[:, :, 8 * g : 8 * g + 8, :].reshape(160, 128) for g in range(4)
    ]
    for quarter, packed in enumerate(block_transpose(groups, lane)):
        packed = packed.reshape(5, 4, 8, 128)
        for plane in range(4):
            pack[4 * plane + quarter] = packed[:, plane]

    pl.semaphore_wait(barrier, 15 + mine_rank)
    each_rank(0, mine_rank, lambda to: signal(slab_ready, to, sec))

    @pl.when(plane_at == 7)
    def _():
        signal(halo_ready.at[1], right, sec)

    def sums_copy(peer, at):
        return remote(sums.at[me], sums.at[me], s_send.at[at], s_recv.at[me], ax, peer)

    def sums_from(at):
        return remote(sums.at[at], sums.at[at], s_send.at[at], s_recv.at[at], ax, sec)

    def pack_copy(peer, at):
        return remote(pack.at[at], recv.at[me], a_send.at[at], a_recv.at[me], ax, peer)

    def pack_from(at):
        return remote(pack.at[at], recv.at[at], a_send.at[at], a_recv.at[at], ax, sec)

    def back_copy(peer, at):
        return remote(send.at[at], back.at[me], b_send.at[at], b_recv.at[me], ax, peer)

    def back_from(at):
        return remote(send.at[at], back.at[at], b_send.at[at], b_recv.at[at], ax, sec)

    def slab_copy(to):
        return remote(slabs.at[ax], slabs.at[ax], t_send.at[to], t_recv.at[ax], to, sec)

    def proxy_copy(to):
        return remote(
            slabs.at[left], slabs.at[left], p_send.at[to], t_recv.at[left], to, sec
        )

    def slab_from(to):
        return remote(slabs.at[to], slabs.at[to], t_send.at[to], t_recv.at[to], to, sec)

    to_right = remote(q_ref, halo.at[0], h_send.at[0], h_recv.at[0], right, sec)
    to_left = remote(q_ref, halo.at[1], h_send.at[1], h_recv.at[1], left, sec)
    second_core = core == 1
    pass_on = remote(q_ref, relay, r_send, r_recv, right, sec)
    carry = remote(q_ref, relay, r_send, r_recv, lax.rem(ax + NAX - 7, NAX), sec)
    forward_right = remote(
        relay, halo.at[0], f_send, h_recv.at[0], lax.rem(ax + 8, NAX), sec
    )
    forward_left = remote(
        relay, halo.at[1], f_send, h_recv.at[1], lax.rem(ax + NAX - 2, NAX), sec
    )

    def at_plane(where, which):
        return jnp.logical_and(plane_at == where, which)

    each_rank(0, mine_rank, lambda to: slab_copy(to).start())

    for peer, at in ordered:
        pack_copy(peer, at).start()

    @pl.when(at_plane(7, second_core))
    def _():
        carry.start()

    @pl.when(plane_at != 0)
    def _():
        signal(halo_ready.at[0], left, sec)

    @pl.when(plane_at != 0)
    def _():
        to_left.start()

    recv[me] = pack[me]

    loads[3].wait()
    whole = [q_ref[c].reshape(128, 128) for c in range(5)]
    v, pressure, heat = physical(whole)
    inverse_radius = rows_ref[1:2, :]
    diffused = v + [heat]
    tend = []
    for c, field in enumerate(flux(whole, v, pressure, 2)):
        value = jnp.dot(
            field, radial_ref[0], precision=HIGHEST, preferred_element_type=F32
        )
        if c:
            value = value + jnp.dot(
                diffused[c - 1],
                radial_ref[2 if c == 4 else 1],
                precision=HIGHEST,
                preferred_element_type=F32,
            )
        tend.append(value)
    turn = TIME_STEP * inverse_radius
    tend[2] = tend[2] - whole[2] * v[2] * turn
    tend[3] = tend[3] + (whole[2] * v[1] + pressure) * turn
    for c in range(5):
        out_ref[c] = tend[c].reshape(4, 32, 128)

    @pl.when(plane_at != 7)
    def _():
        pl.semaphore_wait(halo_ready.at[0], 1)

    @pl.when(plane_at == 0)
    def _():
        slab_copy(right).start()

    @pl.when(plane_at != 7)
    def _():
        to_right.start()

    @pl.when(at_plane(0, second_core))
    def _():
        pass_on.start()

    loads[2].wait()
    loads[4].wait()
    loads[5].wait()
    mine = quarter_ref[lax.rem(me, 4)]

    def columns(which):
        lines = recv[pl.ds(8 * which, 8)]
        lines = [lines[:, c].reshape(64, 128) for c in range(5)]
        v, pressure, heat = physical(lines)
        fields = [f * mine[0:1] for f in flux(lines, v, pressure, 1)]
        viscous = [u * mine[1:2] for u in v] + [heat * mine[2:3]]
        shifts = [fields[0]] + [
            pltpu.roll(fields[0], 128 - 32 * g, 1) for g in range(1, 4)
        ]
        wide = jnp.concatenate(
            [
                jnp.concatenate(block_transpose(fields[1:], lane), axis=0),
                jnp.concatenate(shifts, axis=0),
            ],
            axis=1,
        )
        thin = jnp.concatenate(block_transpose(viscous, lane), axis=0)
        return split(wide), split(thin)

    def product(rows, which, inputs):
        parts = []
        for order, (x_high, x_low) in enumerate(inputs):
            a_high = high[rows, which, order]
            a_low = low[rows, which, order]

            def dot(a, b):
                return jnp.dot(a, b, preferred_element_type=F32)

            parts.append(
                dot(a_high, x_high) + (dot(a_high, x_low) + dot(a_low, x_high))
            )
        wide, thin = parts
        return wide[:, :128] + thin, wide[:, 128:]

    def deliver(rows, main, edge):
        main = [main[64 * g : 64 * g + 64] for g in range(4)]
        edge = [edge[64 * g : 64 * g + 64] for g in range(4)]
        plain = edge[0]
        for g in range(1, 4):
            plain = jnp.where(
                lane // 32 == g, pltpu.roll(edge[g], 32 * g, 1), plain
            )
        for c, value in enumerate((plain,) + tuple(block_transpose(main, lane))):
            send[pl.ds(8 * rows, 8), c] = value.reshape(8, 8, 128)

    for _, at in near_peers:
        pack_from(at).wait_recv()
    inputs = columns(half)
    far_main, far_edge = product(1 - half, half, inputs)
    near_main, near_edge = product(half, half, inputs)

    def slabs_to_later():
        pl.semaphore_wait(slab_ready, NAX - 1 - mine_rank)
        each_rank(mine_rank + 1, NAX, lambda to: slab_copy(to).start())

    @pl.when(plane_at == 1)
    def _():
        slab_from(left).wait_recv()
        each_rank(mine_rank - 3, mine_rank, lambda to: proxy_copy(to).start())

    @pl.when(jnp.logical_and(plane_at != 0, mine_rank < NAX - 1))
    def _():
        slabs_to_later()

    @pl.when(plane_at == 1)
    def _():
        each_rank(mine_rank + 1, NAX, lambda to: proxy_copy(to).start())

    for peer, at in ordered:
        pack_copy(peer, at).wait_send()

    @pl.when(at_plane(7, core == 0))
    def _():
        to_right.start()

    for _, at in far_peers:
        pack_from(at).wait_recv()
    inputs = columns(1 - half)
    main, edge = product(1 - half, 1 - half, inputs)
    deliver(1 - half, far_main + main, far_edge + edge)


    @pl.when(at_plane(7, core == 0))
    def _():
        to_right.wait_send()

    for peer, at in far_peers:
        back_copy(peer, at).start()
    main, edge = product(half, 1 - half, inputs)
    deliver(half, near_main + main, near_edge + edge)
    for peer, at in near_peers:
        back_copy(peer, at).start()
    back[me] = send[me]

    gap = jnp.where(plane_at == 1, 4, 0)
    each_rank(0, mine_rank - gap, lambda to: slab_from(to).wait_recv())
    each_rank(
        mine_rank + jnp.where(plane_at == 1, -3, 1),
        mine_rank,
        lambda to: slab_from(to).wait_recv(),
    )
    each_rank(mine_rank + 1, NAX, lambda to: slab_from(to).wait_recv())
    total = slabs[0]
    for s in range(1, NAX):
        total = total + slabs[s]
    sums[me] = total
    for peer, at in ordered:
        sums_copy(peer, at).start()

    @pl.when(at_plane(0, second_core))
    def _():
        carry.wait_recv()
        forward_right.start()

    for peer, at in ordered:
        back_copy(peer, at).wait_send()

    @pl.when(plane_at == 0)
    def _():
        pl.semaphore_wait(halo_ready.at[1], 1)

    @pl.when(at_plane(0, core == 0))
    def _():
        to_left.start()

    @pl.when(at_plane(1, second_core))
    def _():
        pass_on.wait_recv()
        forward_left.start()

    for _, at in near_peers + far_peers:
        back_from(at).wait_recv()
    ret = [
        jnp.stack([back[4 * p + quarter] for p in range(4)]).reshape(160, 128)
        for quarter in range(4)
    ]
    for g, value in enumerate(block_transpose(ret, lane)):
        value = value.reshape(4, 5, 8, 128)
        rows = slice(8 * g, 8 * g + 8)
        for c in range(5):
            out_ref[c, :, rows, :] = out_ref[c, :, rows, :] + value[:, c]

    to_right.wait_recv()
    to_left.wait_recv()
    planes_flux, planes_visc = [], []
    for block in (halo.at[0], q_ref, halo.at[1]):
        cells = [block[c].reshape(128, 128) for c in range(5)]
        v, pressure, heat = physical(cells)
        fields = [f.reshape(4, 32, 128) for f in flux(cells, v, pressure, 0)]
        others = [f.reshape(4, 32, 128) for f in v + [heat]]
        for plane in range(4):
            planes_flux.append([f[plane] for f in fields])
            planes_visc.append([f[plane] for f in others])
    for plane in range(4):
        at = plane + 4
        for c in range(5):
            value = out_ref[c, plane]
            for k in range(1, 5):
                weight = -TIME_STEP * FIRST_COEFFS[k - 1] / AXIAL_STEP
                value = value + weight * (
                    planes_flux[at + k][c] - planes_flux[at - k][c]
                )
            if c:
                factor = (CONDUCTION if c == 4 else VISCOSITY) * TIME_STEP
                factor = factor / (AXIAL_STEP * AXIAL_STEP)
                value = value + factor * SECOND_CENTER * planes_visc[at][c - 1]
                for k in range(1, 5):
                    value = value + factor * SECOND_COEFFS[k - 1] * (
                        planes_visc[at + k][c - 1] + planes_visc[at - k][c - 1]
                    )
            out_ref[c, plane] = value

    speed = q_ref[1] / q_ref[0]
    for _, at in ordered:
        sums_from(at).wait_recv()
    total = sums[0]
    for s in range(1, NSEC):
        total = total + sums[s]
    bulk = jnp.sum(total, axis=1, keepdims=True) * scale
    forcing = (TIME_STEP * FORCE_RATE) * (TARGET_BULK - bulk)
    forcing = forcing.reshape(1, 1, 1)
    out_ref[1] = out_ref[1] + forcing
    out_ref[4] = out_ref[4] + forcing * speed

    for peer, at in ordered:
        sums_copy(peer, at).wait_send()

    @pl.when(plane_at != 7)
    def _():
        to_right.wait_send()


    @pl.when(jnp.logical_or(plane_at != 0, core == 0))
    def _():
        to_left.wait_send()

    @pl.when(at_plane(0, second_core))
    def _():
        pass_on.wait_send()

    @pl.when(at_plane(7, second_core))
    def _():
        carry.wait_send()

    @pl.when(at_plane(0, second_core))
    def _():
        forward_right.wait_send()

    @pl.when(at_plane(1, second_core))
    def _():
        forward_left.wait_send()

    each_rank(0, mine_rank, lambda to: slab_copy(to).wait_send())

    @pl.when(plane_at == 0)
    def _():
        pl.semaphore_wait(slab_ready, NAX - 1 - mine_rank)
        slab_copy(right).wait_send()

    @pl.when(plane_at != 0)
    def _():
        each_rank(mine_rank + 1, NAX, lambda to: slab_copy(to).wait_send())

    @pl.when(plane_at == 1)
    def _():
        each_rank(mine_rank - 3, mine_rank, lambda to: proxy_copy(to).wait_send())
        each_rank(mine_rank + 1, NAX, lambda to: proxy_copy(to).wait_send())


def solution(mesh):
    high, low, radial, rows, quarter, scale = constants()

    def shards(balance_quantities, register):
        vmem = pl.BlockSpec(memory_space=pltpu.VMEM)
        hbm = pl.BlockSpec(memory_space=pltpu.HBM)
        dma = pltpu.SemaphoreType.DMA
        chunk = pltpu.VMEM((NSEC, 5, 8, 128), F32)
        each = dma((NSEC,))
        operands = (balance_quantities, high, low, radial, rows, quarter)
        tendency = pl.pallas_call(
            functools.partial(body, scale),
            out_shape=jax.ShapeDtypeStruct((5, 4, 32, R), F32),
            in_specs=[hbm] * 6,
            out_specs=vmem,
            scratch_shapes=[pltpu.VMEM(o.shape, o.dtype) for o in operands]
            + [chunk] * 4
            + [
                pltpu.VMEM((2, 5, 4, 32, R), F32),
                pltpu.VMEM((5, 4, 32, R), F32),
                pltpu.VMEM((NSEC, 1, 128), F32),
                pltpu.VMEM((NAX, 1, 128), F32),
                dma((6,)),
                each,
                each,
                each,
                each,
                each,
                each,
                dma((NAX,)),
                dma((NAX,)),
                dma((NAX,)),
                dma((2,)),
                dma((2,)),
                dma,
                dma,
                dma,
                pltpu.SemaphoreType.REGULAR((2,)),
                pltpu.SemaphoreType.REGULAR,
            ],
            compiler_params=pltpu.CompilerParams(
                collective_id=0,
                has_side_effects=True,
                vmem_limit_bytes=60 * 1024 * 1024,
            ),
        )(*operands)
        register_new = SECTION_DECAY * register + tendency
        conserved_new = balance_quantities + SEGMENT_WEIGHT * register_new
        return conserved_new, register_new

    spec = P(None, "ax", "sec", None)
    return jax.shard_map(
        shards,
        mesh=mesh,
        in_specs=(spec, spec),
        out_specs=(spec, spec),
        check_vma=False,
    )
```

```python
import functools

import jax
import jax.numpy as jnp
import ml_dtypes
import numpy as np
from jax import lax
from jax.experimental import pallas as pl
from jax.experimental.pallas import tpu as pltpu
from jax.sharding import PartitionSpec as P

AXIAL_STEP = 0.003
TIME_STEP = 0.001
SECTION_DECAY = -5.0 / 9.0
SEGMENT_WEIGHT = 15.0 / 16.0
VISCOSITY = 2.5e-05
CONDUCTION = VISCOSITY / (0.4 * 0.7)
TARGET_BULK = 0.4
FORCE_RATE = 8000.0
FIRST_COEFFS = (4.0 / 5.0, -1.0 / 5.0, 4.0 / 105.0, -1.0 / 280.0)
SECOND_CENTER = -205.0 / 72.0
SECOND_COEFFS = (8.0 / 5.0, -1.0 / 5.0, 8.0 / 315.0, -1.0 / 560.0)
HIGHEST = lax.Precision.HIGHEST
MESH = pl.DeviceIdType.MESH

R = 128
NTH = 512
NZ = 128
NSEC = 16
NAX = 32
F32 = jnp.float32
BF16 = jnp.bfloat16


def constants():
    index = np.arange(R)
    nodes = np.cos(np.pi * index / (R - 1))
    radius = 0.625 + 0.375 * nodes
    ends = np.where((index == 0) | (index == R - 1), 2.0, 1.0)
    spread = nodes[:, None] - nodes[None, :]
    np.fill_diagonal(spread, 1.0)
    parity = np.where((index[:, None] + index[None, :]) % 2 == 0, 1.0, -1.0)
    off = ends[:, None] / ends[None, :] * parity / spread
    np.fill_diagonal(off, 0.0)
    first = (off - np.diag(off.sum(axis=1))) * (2.0 / 0.75)
    second = first @ first

    lag = (np.arange(NTH)[:, None] - np.arange(NTH)[None, :]) % NTH
    step = 2.0 * np.pi / NTH
    sign = np.where(lag % 2 == 0, 1.0, -1.0)
    safe = np.where(lag == 0, 1, lag)
    azim_first = np.where(lag == 0, 0.0, 0.5 * sign / np.tan(safe * step / 2))
    azim_second = np.where(
        lag == 0,
        -np.pi * np.pi / (3.0 * step * step) - 1.0 / 6.0,
        -0.5 * sign / np.sin(safe * step / 2) ** 2,
    )
    order = np.arange(NTH).reshape(4, 2, 2, 4, 8).transpose(1, 3, 0, 2, 4).reshape(NTH)
    both = np.stack([azim_first[order][:, order], azim_second[order][:, order]])
    both = both.reshape(2, 2, 256, 2, 256).transpose(1, 3, 0, 2, 4)
    both = both.astype(np.float32)
    high = both.astype(ml_dtypes.bfloat16)
    low = (both - high.astype(np.float32)).astype(ml_dtypes.bfloat16)

    flux_op = -TIME_STEP * (first * radius[None, :]) / radius[:, None]
    diff_op = TIME_STEP * (second + first / radius[:, None])
    radial = np.stack(
        [flux_op.T, VISCOSITY * diff_op.T, CONDUCTION * diff_op.T]
    ).astype(np.float32)

    rows = np.zeros((8, R), np.float32)
    rows[0] = radius
    rows[1] = 1.0 / radius
    quarter = np.zeros((4, 8, R), np.float32)
    for q in range(4):
        own = np.tile(radius[32 * q : 32 * q + 32], 4)
        quarter[q, 0] = -TIME_STEP / own
        quarter[q, 1] = TIME_STEP * VISCOSITY / own**2
        quarter[q, 2] = TIME_STEP * CONDUCTION / own**2
    scale = 1.0 / (NZ * NTH * radius.sum())
    return high, low, radial, rows, quarter, float(scale)


def block_transpose(v, lane):
    v0, v1, v2, v3 = v
    low = lane < 64
    even = (lane // 32) % 2 == 0

    def swap(a, b, mask, shift):
        return (
            jnp.where(mask, a, pltpu.roll(b, shift, 1)),
            jnp.where(mask, pltpu.roll(a, 128 - shift, 1), b),
        )

    a0, a2 = swap(v0, v2, low, 64)
    a1, a3 = swap(v1, v3, low, 64)
    b0, b1 = swap(a0, a1, even, 32)
    b2, b3 = swap(a2, a3, even, 32)
    return b0, b1, b2, b3


def physical(q):
    inverse = 1.0 / q[0]
    v = [q[1] * inverse, q[2] * inverse, q[3] * inverse]
    pressure = 0.4 * (q[4] - 0.5 * (q[1] * v[0] + q[2] * v[1] + q[3] * v[2]))
    return v, pressure, pressure * inverse


def flux(q, v, pressure, direction):
    w = v[direction]
    out = [q[1 + direction], q[1] * w, q[2] * w, q[3] * w, (q[4] + pressure) * w]
    out[1 + direction] = out[1 + direction] + pressure
    return out


def split(x):
    high = x.astype(BF16)
    return high, (x - high.astype(F32)).astype(BF16)


def body(
    scale,
    q_hbm,
    high_hbm,
    low_hbm,
    radial_hbm,
    rows_hbm,
    quarter_hbm,
    out_ref,
    q_ref,
    high,
    low,
    radial_ref,
    rows_ref,
    quarter_ref,
    pack,
    recv,
    send,
    back,
    halo,
    relay,
    sums,
    slabs,
    load_sem,
    a_send,
    a_recv,
    s_send,
    s_recv,
    b_send,
    b_recv,
    t_send,
    t_recv,
    p_send,
    h_send,
    h_recv,
    r_send,
    r_recv,
    f_send,
    halo_ready,
    slab_ready,
):
    ax = lax.axis_index("ax")
    sec = lax.axis_index("sec")
    x, half, core = sec // 4, lax.rem(sec // 2, 2), lax.rem(sec, 2)
    me = 8 * half + 2 * x + core

    def remote(src, dst, send_sem, recv_sem, to_ax, to_sec):
        return pltpu.make_async_remote_copy(
            src_ref=src,
            dst_ref=dst,
            send_sem=send_sem,
            recv_sem=recv_sem,
            device_id=(to_ax, to_sec),
            device_id_type=MESH,
        )

    def at_sector(to_x, to_half, to_core):
        return 4 * to_x + 2 * to_half + to_core, 8 * to_half + 2 * to_x + to_core

    def shifted(dx):
        return lax.rem(x + dx, 4)

    far_peers = [
        at_sector(shifted(dx), 1 - half, c) for c in range(2) for dx in (2, 1, 3, 0)
    ]
    near_peers = [
        at_sector(shifted(dx), half, c) for c in range(2) for dx in (2, 1, 3)
    ] + [at_sector(x, half, 1 - core)]
    ordered = far_peers + near_peers

    plane_at = lax.rem(ax, 8)
    right = lax.rem(ax + 1, NAX)
    left = lax.rem(ax + NAX - 1, NAX)

    def rank(at):
        return 4 * lax.rem(at, 8) + at // 8

    def ranked(at):
        return 8 * lax.rem(at, 4) + at // 4

    mine_rank = rank(ax)

    def each_rank(low, high, action):
        lax.fori_loop(low, high, lambda r, _: (action(ranked(r)), 0)[1], 0)

    def signal(sem, to_ax, to_sec):
        pl.semaphore_signal(
            sem, inc=1, device_id=(to_ax, to_sec), device_id_type=MESH
        )

    barrier = pltpu.get_barrier_semaphore()
    loads = [
        pltpu.make_async_copy(src, dst, load_sem.at[i])
        for i, (src, dst) in enumerate(
            (
                (q_hbm, q_ref),
                (rows_hbm, rows_ref),
                (quarter_hbm, quarter_ref),
                (radial_hbm, radial_ref),
                (high_hbm, high),
                (low_hbm, low),
            )
        )
    ]
    loads[0].start()
    loads[1].start()
    for peer, _ in ordered:
        signal(barrier, ax, peer)

    each_rank(mine_rank + 1, NAX, lambda to: signal(barrier, to, sec))
    for copy in loads[2:]:
        copy.start()

    loads[0].wait()
    loads[1].wait()
    radius = rows_ref[0:1, :]
    flow = jnp.sum(q_ref[1].reshape(128, 128) * radius, axis=0, keepdims=True)
    slabs[ax] = flow

    lane = lax.broadcasted_iota(jnp.int32, (1, 128), 1)
    groups = [
        q_ref[:, :, 8 * g : 8 * g + 8, :].reshape(160, 128) for g in range(4)
    ]
    for quarter, packed in enumerate(block_transpose(groups, lane)):
        packed = packed.reshape(5, 4, 8, 128)
        for plane in range(4):
            pack[4 * plane + quarter] = packed[:, plane]

    pl.semaphore_wait(barrier, 15 + mine_rank)
    each_rank(0, mine_rank, lambda to: signal(slab_ready, to, sec))

    @pl.when(plane_at == 7)
    def _():
        signal(halo_ready.at[1], right, sec)

    def sums_copy(peer, at):
        return remote(sums.at[me], sums.at[me], s_send.at[at], s_recv.at[me], ax, peer)

    def sums_from(at):
        return remote(sums.at[at], sums.at[at], s_send.at[at], s_recv.at[at], ax, sec)

    def pack_copy(peer, at):
        return remote(pack.at[at], recv.at[me], a_send.at[at], a_recv.at[me], ax, peer)

    def pack_from(at):
        return remote(pack.at[at], recv.at[at], a_send.at[at], a_recv.at[at], ax, sec)

    def back_copy(peer, at):
        return remote(send.at[at], back.at[me], b_send.at[at], b_recv.at[me], ax, peer)

    def back_from(at):
        return remote(send.at[at], back.at[at], b_send.at[at], b_recv.at[at], ax, sec)

    def slab_copy(to):
        return remote(slabs.at[ax], slabs.at[ax], t_send.at[to], t_recv.at[ax], to, sec)

    def proxy_copy(to):
        return remote(
            slabs.at[left], slabs.at[left], p_send.at[to], t_recv.at[left], to, sec
        )

    def slab_from(to):
        return remote(slabs.at[to], slabs.at[to], t_send.at[to], t_recv.at[to], to, sec)

    to_right = remote(q_ref, halo.at[0], h_send.at[0], h_recv.at[0], right, sec)
    to_left = remote(q_ref, halo.at[1], h_send.at[1], h_recv.at[1], left, sec)
    second_core = core == 1
    pass_on = remote(q_ref, relay, r_send, r_recv, right, sec)
    carry = remote(q_ref, relay, r_send, r_recv, lax.rem(ax + NAX - 7, NAX), sec)
    forward_right = remote(
        relay, halo.at[0], f_send, h_recv.at[0], lax.rem(ax + 8, NAX), sec
    )
    forward_left = remote(
        relay, halo.at[1], f_send, h_recv.at[1], lax.rem(ax + NAX - 2, NAX), sec
    )

    def at_plane(where, which):
        return jnp.logical_and(plane_at == where, which)

    each_rank(0, mine_rank, lambda to: slab_copy(to).start())

    for peer, at in ordered:
        pack_copy(peer, at).start()

    @pl.when(at_plane(7, core == 0))
    def _():
        to_right.start()

    @pl.when(at_plane(7, second_core))
    def _():
        carry.start()

    @pl.when(plane_at != 0)
    def _():
        signal(halo_ready.at[0], left, sec)

    @pl.when(plane_at != 0)
    def _():
        to_left.start()

    recv[me] = pack[me]

    loads[3].wait()
    whole = [q_ref[c].reshape(128, 128) for c in range(5)]
    v, pressure, heat = physical(whole)
    inverse_radius = rows_ref[1:2, :]
    diffused = v + [heat]
    tend = []
    for c, field in enumerate(flux(whole, v, pressure, 2)):
        value = jnp.dot(
            field, radial_ref[0], precision=HIGHEST, preferred_element_type=F32
        )
        if c:
            value = value + jnp.dot(
                diffused[c - 1],
                radial_ref[2 if c == 4 else 1],
                precision=HIGHEST,
                preferred_element_type=F32,
            )
        tend.append(value)
    turn = TIME_STEP * inverse_radius
    tend[2] = tend[2] - whole[2] * v[2] * turn
    tend[3] = tend[3] + (whole[2] * v[1] + pressure) * turn
    for c in range(5):
        out_ref[c] = tend[c].reshape(4, 32, 128)

    @pl.when(plane_at != 7)
    def _():
        pl.semaphore_wait(halo_ready.at[0], 1)

    @pl.when(plane_at == 0)
    def _():
        slab_copy(right).start()

    @pl.when(plane_at != 7)
    def _():
        to_right.start()

    @pl.when(at_plane(0, second_core))
    def _():
        pass_on.start()

    loads[2].wait()
    loads[4].wait()
    loads[5].wait()
    mine = quarter_ref[lax.rem(me, 4)]

    def columns(which):
        lines = recv[pl.ds(8 * which, 8)]
        lines = [lines[:, c].reshape(64, 128) for c in range(5)]
        v, pressure, heat = physical(lines)
        fields = [f * mine[0:1] for f in flux(lines, v, pressure, 1)]
        viscous = [u * mine[1:2] for u in v] + [heat * mine[2:3]]
        shifts = [fields[0]] + [
            pltpu.roll(fields[0], 128 - 32 * g, 1) for g in range(1, 4)
        ]
        wide = jnp.concatenate(
            [
                jnp.concatenate(block_transpose(fields[1:], lane), axis=0),
                jnp.concatenate(shifts, axis=0),
            ],
            axis=1,
        )
        thin = jnp.concatenate(block_transpose(viscous, lane), axis=0)
        return split(wide), split(thin)

    def product(rows, which, inputs):
        parts = []
        for order, (x_high, x_low) in enumerate(inputs):
            a_high = high[rows, which, order]
            a_low = low[rows, which, order]

            def dot(a, b):
                return jnp.dot(a, b, preferred_element_type=F32)

            parts.append(
                dot(a_high, x_high) + (dot(a_high, x_low) + dot(a_low, x_high))
            )
        wide, thin = parts
        return wide[:, :128] + thin, wide[:, 128:]

    def deliver(rows, main, edge):
        main = [main[64 * g : 64 * g + 64] for g in range(4)]
        edge = [edge[64 * g : 64 * g + 64] for g in range(4)]
        plain = edge[0]
        for g in range(1, 4):
            plain = jnp.where(
                lane // 32 == g, pltpu.roll(edge[g], 32 * g, 1), plain
            )
        for c, value in enumerate((plain,) + tuple(block_transpose(main, lane))):
            send[pl.ds(8 * rows, 8), c] = value.reshape(8, 8, 128)

    for _, at in near_peers:
        pack_from(at).wait_recv()
    inputs = columns(half)
    far_main, far_edge = product(1 - half, half, inputs)
    near_main, near_edge = product(half, half, inputs)

    def slabs_to_later():
        pl.semaphore_wait(slab_ready, NAX - 1 - mine_rank)
        each_rank(mine_rank + 1, NAX, lambda to: slab_copy(to).start())

    @pl.when(plane_at == 1)
    def _():
        slab_from(left).wait_recv()
        each_rank(mine_rank - 3, mine_rank, lambda to: proxy_copy(to).start())

    @pl.when(jnp.logical_and(plane_at != 0, mine_rank < NAX - 1))
    def _():
        slabs_to_later()

    @pl.when(plane_at == 1)
    def _():
        each_rank(mine_rank + 1, NAX, lambda to: proxy_copy(to).start())

    for peer, at in ordered:
        pack_copy(peer, at).wait_send()

    for _, at in far_peers:
        pack_from(at).wait_recv()
    inputs = columns(1 - half)
    main, edge = product(1 - half, 1 - half, inputs)
    deliver(1 - half, far_main + main, far_edge + edge)


    @pl.when(at_plane(7, core == 0))
    def _():
        to_right.wait_send()

    for peer, at in far_peers:
        back_copy(peer, at).start()
    main, edge = product(half, 1 - half, inputs)
    deliver(half, near_main + main, near_edge + edge)
    for peer, at in near_peers:
        back_copy(peer, at).start()
    back[me] = send[me]

    gap = jnp.where(plane_at == 1, 4, 0)
    each_rank(0, mine_rank - gap, lambda to: slab_from(to).wait_recv())
    each_rank(
        mine_rank + jnp.where(plane_at == 1, -3, 1),
        mine_rank,
        lambda to: slab_from(to).wait_recv(),
    )
    each_rank(mine_rank + 1, NAX, lambda to: slab_from(to).wait_recv())
    total = slabs[0]
    for s in range(1, NAX):
        total = total + slabs[s]
    sums[me] = total
    for peer, at in ordered:
        sums_copy(peer, at).start()

    @pl.when(at_plane(0, second_core))
    def _():
        carry.wait_recv()
        forward_right.start()

    for peer, at in ordered:
        back_copy(peer, at).wait_send()

    @pl.when(plane_at == 0)
    def _():
        pl.semaphore_wait(halo_ready.at[1], 1)

    @pl.when(at_plane(0, core == 0))
    def _():
        to_left.start()

    @pl.when(at_plane(1, second_core))
    def _():
        pass_on.wait_recv()
        forward_left.start()

    for _, at in near_peers + far_peers:
        back_from(at).wait_recv()
    ret = [
        jnp.stack([back[4 * p + quarter] for p in range(4)]).reshape(160, 128)
        for quarter in range(4)
    ]
    for g, value in enumerate(block_transpose(ret, lane)):
        value = value.reshape(4, 5, 8, 128)
        rows = slice(8 * g, 8 * g + 8)
        for c in range(5):
            out_ref[c, :, rows, :] = out_ref[c, :, rows, :] + value[:, c]

    to_right.wait_recv()
    to_left.wait_recv()
    planes_flux, planes_visc = [], []
    for block in (halo.at[0], q_ref, halo.at[1]):
        cells = [block[c].reshape(128, 128) for c in range(5)]
        v, pressure, heat = physical(cells)
        fields = [f.reshape(4, 32, 128) for f in flux(cells, v, pressure, 0)]
        others = [f.reshape(4, 32, 128) for f in v + [heat]]
        for plane in range(4):
            planes_flux.append([f[plane] for f in fields])
            planes_visc.append([f[plane] for f in others])
    for plane in range(4):
        at = plane + 4
        for c in range(5):
            value = out_ref[c, plane]
            for k in range(1, 5):
                weight = -TIME_STEP * FIRST_COEFFS[k - 1] / AXIAL_STEP
                value = value + weight * (
                    planes_flux[at + k][c] - planes_flux[at - k][c]
                )
            if c:
                factor = (CONDUCTION if c == 4 else VISCOSITY) * TIME_STEP
                factor = factor / (AXIAL_STEP * AXIAL_STEP)
                value = value + factor * SECOND_CENTER * planes_visc[at][c - 1]
                for k in range(1, 5):
                    value = value + factor * SECOND_COEFFS[k - 1] * (
                        planes_visc[at + k][c - 1] + planes_visc[at - k][c - 1]
                    )
            out_ref[c, plane] = value

    speed = q_ref[1] / q_ref[0]
    for _, at in ordered:
        sums_from(at).wait_recv()
    total = sums[0]
    for s in range(1, NSEC):
        total = total + sums[s]
    bulk = jnp.sum(total, axis=1, keepdims=True) * scale
    forcing = (TIME_STEP * FORCE_RATE) * (TARGET_BULK - bulk)
    forcing = forcing.reshape(1, 1, 1)
    out_ref[1] = out_ref[1] + forcing
    out_ref[4] = out_ref[4] + forcing * speed

    for peer, at in ordered:
        sums_copy(peer, at).wait_send()

    @pl.when(plane_at != 7)
    def _():
        to_right.wait_send()


    @pl.when(jnp.logical_or(plane_at != 0, core == 0))
    def _():
        to_left.wait_send()

    @pl.when(at_plane(0, second_core))
    def _():
        pass_on.wait_send()

    @pl.when(at_plane(7, second_core))
    def _():
        carry.wait_send()

    @pl.when(at_plane(0, second_core))
    def _():
        forward_right.wait_send()

    @pl.when(at_plane(1, second_core))
    def _():
        forward_left.wait_send()

    each_rank(0, mine_rank, lambda to: slab_copy(to).wait_send())

    @pl.when(plane_at == 0)
    def _():
        pl.semaphore_wait(slab_ready, NAX - 1 - mine_rank)
        slab_copy(right).wait_send()

    @pl.when(plane_at != 0)
    def _():
        each_rank(mine_rank + 1, NAX, lambda to: slab_copy(to).wait_send())

    @pl.when(plane_at == 1)
    def _():
        each_rank(mine_rank - 3, mine_rank, lambda to: proxy_copy(to).wait_send())
        each_rank(mine_rank + 1, NAX, lambda to: proxy_copy(to).wait_send())


def solution(mesh):
    high, low, radial, rows, quarter, scale = constants()

    def shards(balance_quantities, register):
        vmem = pl.BlockSpec(memory_space=pltpu.VMEM)
        hbm = pl.BlockSpec(memory_space=pltpu.HBM)
        dma = pltpu.SemaphoreType.DMA
        chunk = pltpu.VMEM((NSEC, 5, 8, 128), F32)
        each = dma((NSEC,))
        operands = (balance_quantities, high, low, radial, rows, quarter)
        tendency = pl.pallas_call(
            functools.partial(body, scale),
            out_shape=jax.ShapeDtypeStruct((5, 4, 32, R), F32),
            in_specs=[hbm] * 6,
            out_specs=vmem,
            scratch_shapes=[pltpu.VMEM(o.shape, o.dtype) for o in operands]
            + [chunk] * 4
            + [
                pltpu.VMEM((2, 5, 4, 32, R), F32),
                pltpu.VMEM((5, 4, 32, R), F32),
                pltpu.VMEM((NSEC, 1, 128), F32),
                pltpu.VMEM((NAX, 1, 128), F32),
                dma((6,)),
                each,
                each,
                each,
                each,
                each,
                each,
                dma((NAX,)),
                dma((NAX,)),
                dma((NAX,)),
                dma((2,)),
                dma((2,)),
                dma,
                dma,
                dma,
                pltpu.SemaphoreType.REGULAR((2,)),
                pltpu.SemaphoreType.REGULAR,
            ],
            compiler_params=pltpu.CompilerParams(
                collective_id=0,
                has_side_effects=True,
                vmem_limit_bytes=60 * 1024 * 1024,
            ),
        )(*operands)
        register_new = SECTION_DECAY * register + tendency
        conserved_new = balance_quantities + SEGMENT_WEIGHT * register_new
        return conserved_new, register_new

    spec = P(None, "ax", "sec", None)
    return jax.shard_map(
        shards,
        mesh=mesh,
        in_specs=(spec, spec),
        out_specs=(spec, spec),
        check_vma=False,
    )
```

```python
import functools

import jax
import jax.numpy as jnp
import ml_dtypes
import numpy as np
from jax import lax
from jax.experimental import pallas as pl
from jax.experimental.pallas import tpu as pltpu
from jax.sharding import PartitionSpec as P

AXIAL_STEP = 0.003
TIME_STEP = 0.001
SECTION_DECAY = -5.0 / 9.0
SEGMENT_WEIGHT = 15.0 / 16.0
VISCOSITY = 2.5e-05
CONDUCTION = VISCOSITY / (0.4 * 0.7)
TARGET_BULK = 0.4
FORCE_RATE = 8000.0
FIRST_COEFFS = (4.0 / 5.0, -1.0 / 5.0, 4.0 / 105.0, -1.0 / 280.0)
SECOND_CENTER = -205.0 / 72.0
SECOND_COEFFS = (8.0 / 5.0, -1.0 / 5.0, 8.0 / 315.0, -1.0 / 560.0)
HIGHEST = lax.Precision.HIGHEST
MESH = pl.DeviceIdType.MESH

R = 128
NTH = 512
NZ = 128
NSEC = 16
NAX = 32
F32 = jnp.float32
BF16 = jnp.bfloat16


def constants():
    index = np.arange(R)
    nodes = np.cos(np.pi * index / (R - 1))
    radius = 0.625 + 0.375 * nodes
    ends = np.where((index == 0) | (index == R - 1), 2.0, 1.0)
    spread = nodes[:, None] - nodes[None, :]
    np.fill_diagonal(spread, 1.0)
    parity = np.where((index[:, None] + index[None, :]) % 2 == 0, 1.0, -1.0)
    off = ends[:, None] / ends[None, :] * parity / spread
    np.fill_diagonal(off, 0.0)
    first = (off - np.diag(off.sum(axis=1))) * (2.0 / 0.75)
    second = first @ first

    lag = (np.arange(NTH)[:, None] - np.arange(NTH)[None, :]) % NTH
    step = 2.0 * np.pi / NTH
    sign = np.where(lag % 2 == 0, 1.0, -1.0)
    safe = np.where(lag == 0, 1, lag)
    azim_first = np.where(lag == 0, 0.0, 0.5 * sign / np.tan(safe * step / 2))
    azim_second = np.where(
        lag == 0,
        -np.pi * np.pi / (3.0 * step * step) - 1.0 / 6.0,
        -0.5 * sign / np.sin(safe * step / 2) ** 2,
    )
    order = np.arange(NTH).reshape(4, 2, 2, 4, 8).transpose(1, 3, 0, 2, 4).reshape(NTH)
    both = np.stack([azim_first[order][:, order], azim_second[order][:, order]])
    both = both.reshape(2, 2, 256, 2, 256).transpose(1, 3, 0, 2, 4)
    both = both.astype(np.float32)
    high = both.astype(ml_dtypes.bfloat16)
    low = (both - high.astype(np.float32)).astype(ml_dtypes.bfloat16)

    flux_op = -TIME_STEP * (first * radius[None, :]) / radius[:, None]
    diff_op = TIME_STEP * (second + first / radius[:, None])
    radial = np.stack(
        [flux_op.T, VISCOSITY * diff_op.T, CONDUCTION * diff_op.T]
    ).astype(np.float32)

    rows = np.zeros((8, R), np.float32)
    rows[0] = radius
    rows[1] = 1.0 / radius
    quarter = np.zeros((4, 8, R), np.float32)
    for q in range(4):
        own = np.tile(radius[32 * q : 32 * q + 32], 4)
        quarter[q, 0] = -TIME_STEP / own
        quarter[q, 1] = TIME_STEP * VISCOSITY / own**2
        quarter[q, 2] = TIME_STEP * CONDUCTION / own**2
    scale = 1.0 / (NZ * NTH * radius.sum())
    return high, low, radial, rows, quarter, float(scale)


def block_transpose(v, lane):
    v0, v1, v2, v3 = v
    low = lane < 64
    even = (lane // 32) % 2 == 0

    def swap(a, b, mask, shift):
        return (
            jnp.where(mask, a, pltpu.roll(b, shift, 1)),
            jnp.where(mask, pltpu.roll(a, 128 - shift, 1), b),
        )

    a0, a2 = swap(v0, v2, low, 64)
    a1, a3 = swap(v1, v3, low, 64)
    b0, b1 = swap(a0, a1, even, 32)
    b2, b3 = swap(a2, a3, even, 32)
    return b0, b1, b2, b3


def physical(q):
    inverse = 1.0 / q[0]
    v = [q[1] * inverse, q[2] * inverse, q[3] * inverse]
    pressure = 0.4 * (q[4] - 0.5 * (q[1] * v[0] + q[2] * v[1] + q[3] * v[2]))
    return v, pressure, pressure * inverse


def flux(q, v, pressure, direction):
    w = v[direction]
    out = [q[1 + direction], q[1] * w, q[2] * w, q[3] * w, (q[4] + pressure) * w]
    out[1 + direction] = out[1 + direction] + pressure
    return out


def split(x):
    high = x.astype(BF16)
    return high, (x - high.astype(F32)).astype(BF16)


def body(
    scale,
    q_hbm,
    high_hbm,
    low_hbm,
    radial_hbm,
    rows_hbm,
    quarter_hbm,
    out_ref,
    q_ref,
    high,
    low,
    radial_ref,
    rows_ref,
    quarter_ref,
    pack,
    recv,
    send,
    back,
    halo,
    relay,
    sums,
    slabs,
    load_sem,
    a_send,
    a_recv,
    s_send,
    s_recv,
    b_send,
    b_recv,
    t_send,
    t_recv,
    p_send,
    h_send,
    h_recv,
    r_send,
    r_recv,
    f_send,
    halo_ready,
    slab_ready,
):
    ax = lax.axis_index("ax")
    sec = lax.axis_index("sec")
    x, half, core = sec // 4, lax.rem(sec // 2, 2), lax.rem(sec, 2)
    me = 8 * half + 2 * x + core

    def remote(src, dst, send_sem, recv_sem, to_ax, to_sec):
        return pltpu.make_async_remote_copy(
            src_ref=src,
            dst_ref=dst,
            send_sem=send_sem,
            recv_sem=recv_sem,
            device_id=(to_ax, to_sec),
            device_id_type=MESH,
        )

    def at_sector(to_x, to_half, to_core):
        return 4 * to_x + 2 * to_half + to_core, 8 * to_half + 2 * to_x + to_core

    def shifted(dx):
        return lax.rem(x + dx, 4)

    far_peers = [
        at_sector(shifted(dx), 1 - half, c) for c in range(2) for dx in (2, 1, 3, 0)
    ]
    near_peers = [
        at_sector(shifted(dx), half, c) for c in range(2) for dx in (2, 1, 3)
    ] + [at_sector(x, half, 1 - core)]
    ordered = far_peers + near_peers

    plane_at = lax.rem(ax, 8)
    right = lax.rem(ax + 1, NAX)
    left = lax.rem(ax + NAX - 1, NAX)

    def rank(at):
        return 4 * lax.rem(at, 8) + at // 8

    def ranked(at):
        return 8 * lax.rem(at, 4) + at // 4

    mine_rank = rank(ax)

    def each_rank(low, high, action):
        lax.fori_loop(low, high, lambda r, _: (action(ranked(r)), 0)[1], 0)

    def signal(sem, to_ax, to_sec):
        pl.semaphore_signal(
            sem, inc=1, device_id=(to_ax, to_sec), device_id_type=MESH
        )

    barrier = pltpu.get_barrier_semaphore()
    loads = [
        pltpu.make_async_copy(src, dst, load_sem.at[i])
        for i, (src, dst) in enumerate(
            (
                (q_hbm, q_ref),
                (rows_hbm, rows_ref),
                (quarter_hbm, quarter_ref),
                (radial_hbm, radial_ref),
                (high_hbm, high),
                (low_hbm, low),
            )
        )
    ]
    loads[0].start()
    loads[1].start()
    for peer, _ in ordered:
        signal(barrier, ax, peer)

    each_rank(mine_rank + 1, NAX, lambda to: signal(barrier, to, sec))
    for copy in loads[2:]:
        copy.start()

    loads[0].wait()
    loads[1].wait()
    radius = rows_ref[0:1, :]
    flow = jnp.sum(q_ref[1].reshape(128, 128) * radius, axis=0, keepdims=True)
    slabs[ax] = flow

    lane = lax.broadcasted_iota(jnp.int32, (1, 128), 1)
    groups = [
        q_ref[:, :, 8 * g : 8 * g + 8, :].reshape(160, 128) for g in range(4)
    ]
    for quarter, packed in enumerate(block_transpose(groups, lane)):
        packed = packed.reshape(5, 4, 8, 128)
        for plane in range(4):
            pack[4 * plane + quarter] = packed[:, plane]

    pl.semaphore_wait(barrier, 15 + mine_rank)
    each_rank(0, mine_rank, lambda to: signal(slab_ready, to, sec))

    @pl.when(plane_at == 7)
    def _():
        signal(halo_ready.at[1], right, sec)

    def sums_copy(peer, at):
        return remote(sums.at[me], sums.at[me], s_send.at[at], s_recv.at[me], ax, peer)

    def sums_from(at):
        return remote(sums.at[at], sums.at[at], s_send.at[at], s_recv.at[at], ax, sec)

    def pack_copy(peer, at):
        return remote(pack.at[at], recv.at[me], a_send.at[at], a_recv.at[me], ax, peer)

    def pack_from(at):
        return remote(pack.at[at], recv.at[at], a_send.at[at], a_recv.at[at], ax, sec)

    def back_copy(peer, at):
        return remote(send.at[at], back.at[me], b_send.at[at], b_recv.at[me], ax, peer)

    def back_from(at):
        return remote(send.at[at], back.at[at], b_send.at[at], b_recv.at[at], ax, sec)

    def slab_copy(to):
        return remote(slabs.at[ax], slabs.at[ax], t_send.at[to], t_recv.at[ax], to, sec)

    def proxy_copy(to):
        return remote(
            slabs.at[left], slabs.at[left], p_send.at[to], t_recv.at[left], to, sec
        )

    def slab_from(to):
        return remote(slabs.at[to], slabs.at[to], t_send.at[to], t_recv.at[to], to, sec)

    to_right = remote(q_ref, halo.at[0], h_send.at[0], h_recv.at[0], right, sec)
    to_left = remote(q_ref, halo.at[1], h_send.at[1], h_recv.at[1], left, sec)
    second_core = core == 1
    pass_on = remote(q_ref, relay, r_send, r_recv, right, sec)
    carry = remote(q_ref, relay, r_send, r_recv, lax.rem(ax + NAX - 7, NAX), sec)
    forward_right = remote(
        relay, halo.at[0], f_send, h_recv.at[0], lax.rem(ax + 8, NAX), sec
    )
    forward_left = remote(
        relay, halo.at[1], f_send, h_recv.at[1], lax.rem(ax + NAX - 2, NAX), sec
    )

    def at_plane(where, which):
        return jnp.logical_and(plane_at == where, which)

    each_rank(0, mine_rank, lambda to: slab_copy(to).start())

    for peer, at in ordered:
        pack_copy(peer, at).start()

    @pl.when(at_plane(7, core == 0))
    def _():
        to_right.start()

    @pl.when(at_plane(7, second_core))
    def _():
        carry.start()

    @pl.when(plane_at != 0)
    def _():
        signal(halo_ready.at[0], left, sec)

    @pl.when(plane_at != 0)
    def _():
        to_left.start()

    recv[me] = pack[me]

    loads[3].wait()
    whole = [q_ref[c].reshape(128, 128) for c in range(5)]
    v, pressure, heat = physical(whole)
    inverse_radius = rows_ref[1:2, :]
    diffused = v + [heat]
    tend = []
    for c, field in enumerate(flux(whole, v, pressure, 2)):
        value = jnp.dot(
            field, radial_ref[0], precision=HIGHEST, preferred_element_type=F32
        )
        if c:
            value = value + jnp.dot(
                diffused[c - 1],
                radial_ref[2 if c == 4 else 1],
                precision=HIGHEST,
                preferred_element_type=F32,
            )
        tend.append(value)
    turn = TIME_STEP * inverse_radius
    tend[2] = tend[2] - whole[2] * v[2] * turn
    tend[3] = tend[3] + (whole[2] * v[1] + pressure) * turn
    for c in range(5):
        out_ref[c] = tend[c].reshape(4, 32, 128)

    @pl.when(plane_at != 7)
    def _():
        pl.semaphore_wait(halo_ready.at[0], 1)

    @pl.when(plane_at == 0)
    def _():
        slab_copy(right).start()

    @pl.when(plane_at != 7)
    def _():
        to_right.start()

    @pl.when(at_plane(0, second_core))
    def _():
        pass_on.start()

    loads[2].wait()
    loads[4].wait()
    loads[5].wait()
    mine = quarter_ref[lax.rem(me, 4)]

    def columns(which):
        lines = recv[pl.ds(8 * which, 8)]
        lines = [lines[:, c].reshape(64, 128) for c in range(5)]
        v, pressure, heat = physical(lines)
        fields = [f * mine[0:1] for f in flux(lines, v, pressure, 1)]
        viscous = [u * mine[1:2] for u in v] + [heat * mine[2:3]]
        shifts = [fields[0]] + [
            pltpu.roll(fields[0], 128 - 32 * g, 1) for g in range(1, 4)
        ]
        wide = jnp.concatenate(
            [
                jnp.concatenate(block_transpose(fields[1:], lane), axis=0),
                jnp.concatenate(shifts, axis=0),
            ],
            axis=1,
        )
        thin = jnp.concatenate(block_transpose(viscous, lane), axis=0)
        return split(wide), split(thin)

    def product(rows, which, inputs):
        parts = []
        for order, (x_high, x_low) in enumerate(inputs):
            a_high = high[rows, which, order]
            a_low = low[rows, which, order]

            def dot(a, b):
                return jnp.dot(a, b, preferred_element_type=F32)

            parts.append(
                dot(a_high, x_high) + (dot(a_high, x_low) + dot(a_low, x_high))
            )
        wide, thin = parts
        return wide[:, :128] + thin, wide[:, 128:]

    def deliver(rows, main, edge):
        main = [main[64 * g : 64 * g + 64] for g in range(4)]
        edge = [edge[64 * g : 64 * g + 64] for g in range(4)]
        plain = edge[0]
        for g in range(1, 4):
            plain = jnp.where(
                lane // 32 == g, pltpu.roll(edge[g], 32 * g, 1), plain
            )
        for c, value in enumerate((plain,) + tuple(block_transpose(main, lane))):
            send[pl.ds(8 * rows, 8), c] = value.reshape(8, 8, 128)

    for _, at in near_peers:
        pack_from(at).wait_recv()
    inputs = columns(half)
    far_main, far_edge = product(1 - half, half, inputs)
    near_main, near_edge = product(half, half, inputs)

    def slabs_to_later():
        pl.semaphore_wait(slab_ready, NAX - 1 - mine_rank)
        each_rank(mine_rank + 1, NAX, lambda to: slab_copy(to).start())

    @pl.when(plane_at == 1)
    def _():
        slab_from(left).wait_recv()
        each_rank(mine_rank - 3, mine_rank, lambda to: proxy_copy(to).start())

    @pl.when(jnp.logical_and(plane_at != 0, mine_rank < NAX - 1))
    def _():
        slabs_to_later()

    @pl.when(plane_at == 1)
    def _():
        each_rank(mine_rank + 1, NAX, lambda to: proxy_copy(to).start())

    for peer, at in ordered:
        pack_copy(peer, at).wait_send()

    for _, at in far_peers:
        pack_from(at).wait_recv()
    inputs = columns(1 - half)
    main, edge = product(1 - half, 1 - half, inputs)
    deliver(1 - half, far_main + main, far_edge + edge)


    @pl.when(at_plane(7, core == 0))
    def _():
        to_right.wait_send()

    for peer, at in far_peers:
        back_copy(peer, at).start()
    main, edge = product(half, 1 - half, inputs)
    deliver(half, near_main + main, near_edge + edge)
    for peer, at in near_peers:
        back_copy(peer, at).start()
    back[me] = send[me]

    gap = jnp.where(plane_at == 1, 4, 0)
    each_rank(0, mine_rank - gap, lambda to: slab_from(to).wait_recv())
    each_rank(
        mine_rank + jnp.where(plane_at == 1, -3, 1),
        mine_rank,
        lambda to: slab_from(to).wait_recv(),
    )
    each_rank(mine_rank + 1, NAX, lambda to: slab_from(to).wait_recv())
    total = slabs[0]
    for s in range(1, NAX):
        total = total + slabs[s]
    sums[me] = total
    for peer, at in ordered:
        sums_copy(peer, at).start()

    @pl.when(at_plane(0, second_core))
    def _():
        carry.wait_recv()
        forward_right.start()

    @pl.when(plane_at == 0)
    def _():
        pl.semaphore_wait(halo_ready.at[1], 1)

    @pl.when(at_plane(0, core == 0))
    def _():
        to_left.start()

    @pl.when(at_plane(1, second_core))
    def _():
        pass_on.wait_recv()
        forward_left.start()

    for _, at in near_peers + far_peers:
        back_from(at).wait_recv()
    ret = [
        jnp.stack([back[4 * p + quarter] for p in range(4)]).reshape(160, 128)
        for quarter in range(4)
    ]
    for g, value in enumerate(block_transpose(ret, lane)):
        value = value.reshape(4, 5, 8, 128)
        rows = slice(8 * g, 8 * g + 8)
        for c in range(5):
            out_ref[c, :, rows, :] = out_ref[c, :, rows, :] + value[:, c]

    to_right.wait_recv()
    to_left.wait_recv()
    planes_flux, planes_visc = [], []
    for block in (halo.at[0], q_ref, halo.at[1]):
        cells = [block[c].reshape(128, 128) for c in range(5)]
        v, pressure, heat = physical(cells)
        fields = [f.reshape(4, 32, 128) for f in flux(cells, v, pressure, 0)]
        others = [f.reshape(4, 32, 128) for f in v + [heat]]
        for plane in range(4):
            planes_flux.append([f[plane] for f in fields])
            planes_visc.append([f[plane] for f in others])
    for plane in range(4):
        at = plane + 4
        for c in range(5):
            value = out_ref[c, plane]
            for k in range(1, 5):
                weight = -TIME_STEP * FIRST_COEFFS[k - 1] / AXIAL_STEP
                value = value + weight * (
                    planes_flux[at + k][c] - planes_flux[at - k][c]
                )
            if c:
                factor = (CONDUCTION if c == 4 else VISCOSITY) * TIME_STEP
                factor = factor / (AXIAL_STEP * AXIAL_STEP)
                value = value + factor * SECOND_CENTER * planes_visc[at][c - 1]
                for k in range(1, 5):
                    value = value + factor * SECOND_COEFFS[k - 1] * (
                        planes_visc[at + k][c - 1] + planes_visc[at - k][c - 1]
                    )
            out_ref[c, plane] = value

    speed = q_ref[1] / q_ref[0]
    for _, at in ordered:
        sums_from(at).wait_recv()
    total = sums[0]
    for s in range(1, NSEC):
        total = total + sums[s]
    bulk = jnp.sum(total, axis=1, keepdims=True) * scale
    forcing = (TIME_STEP * FORCE_RATE) * (TARGET_BULK - bulk)
    forcing = forcing.reshape(1, 1, 1)
    out_ref[1] = out_ref[1] + forcing
    out_ref[4] = out_ref[4] + forcing * speed

    for peer, at in ordered:
        sums_copy(peer, at).wait_send()
        back_copy(peer, at).wait_send()

    @pl.when(plane_at != 7)
    def _():
        to_right.wait_send()


    @pl.when(jnp.logical_or(plane_at != 0, core == 0))
    def _():
        to_left.wait_send()

    @pl.when(at_plane(0, second_core))
    def _():
        pass_on.wait_send()

    @pl.when(at_plane(7, second_core))
    def _():
        carry.wait_send()

    @pl.when(at_plane(0, second_core))
    def _():
        forward_right.wait_send()

    @pl.when(at_plane(1, second_core))
    def _():
        forward_left.wait_send()

    each_rank(0, mine_rank, lambda to: slab_copy(to).wait_send())

    @pl.when(plane_at == 0)
    def _():
        pl.semaphore_wait(slab_ready, NAX - 1 - mine_rank)
        slab_copy(right).wait_send()

    @pl.when(plane_at != 0)
    def _():
        each_rank(mine_rank + 1, NAX, lambda to: slab_copy(to).wait_send())

    @pl.when(plane_at == 1)
    def _():
        each_rank(mine_rank - 3, mine_rank, lambda to: proxy_copy(to).wait_send())
        each_rank(mine_rank + 1, NAX, lambda to: proxy_copy(to).wait_send())


def solution(mesh):
    high, low, radial, rows, quarter, scale = constants()

    def shards(balance_quantities, register):
        vmem = pl.BlockSpec(memory_space=pltpu.VMEM)
        hbm = pl.BlockSpec(memory_space=pltpu.HBM)
        dma = pltpu.SemaphoreType.DMA
        chunk = pltpu.VMEM((NSEC, 5, 8, 128), F32)
        each = dma((NSEC,))
        operands = (balance_quantities, high, low, radial, rows, quarter)
        tendency = pl.pallas_call(
            functools.partial(body, scale),
            out_shape=jax.ShapeDtypeStruct((5, 4, 32, R), F32),
            in_specs=[hbm] * 6,
            out_specs=vmem,
            scratch_shapes=[pltpu.VMEM(o.shape, o.dtype) for o in operands]
            + [chunk] * 4
            + [
                pltpu.VMEM((2, 5, 4, 32, R), F32),
                pltpu.VMEM((5, 4, 32, R), F32),
                pltpu.VMEM((NSEC, 1, 128), F32),
                pltpu.VMEM((NAX, 1, 128), F32),
                dma((6,)),
                each,
                each,
                each,
                each,
                each,
                each,
                dma((NAX,)),
                dma((NAX,)),
                dma((NAX,)),
                dma((2,)),
                dma((2,)),
                dma,
                dma,
                dma,
                pltpu.SemaphoreType.REGULAR((2,)),
                pltpu.SemaphoreType.REGULAR,
            ],
            compiler_params=pltpu.CompilerParams(
                collective_id=0,
                has_side_effects=True,
                vmem_limit_bytes=60 * 1024 * 1024,
            ),
        )(*operands)
        register_new = SECTION_DECAY * register + tendency
        conserved_new = balance_quantities + SEGMENT_WEIGHT * register_new
        return conserved_new, register_new

    spec = P(None, "ax", "sec", None)
    return jax.shard_map(
        shards,
        mesh=mesh,
        in_specs=(spec, spec),
        out_specs=(spec, spec),
        check_vma=False,
    )
```
